32 devices in a mesh: dp: 8 (over z, x), fsdp: 4 (over y, core).
Axes of the slice: x: 2, y: 2, z: 4, core: 2. Of those that a mesh axis runs over, the one named last changes fastest.
Arguments:
- tokens: bfloat16 [16384, 960], P(('dp', 'fsdp')), may hold values from -6 to 6
- norm_gains: bfloat16 [2, 960], P(None, 'dp'), may hold values from 0.5 to 1.5
- query_weight: bfloat16 [960, 960], P('fsdp', 'dp'), may hold values from -0.1875 to 0.1875
- key_weight: bfloat16 [960, 320], P('fsdp', 'dp'), may hold values from -0.1875 to 0.1875
- value_weight: bfloat16 [960, 320], P('fsdp', 'dp'), may hold values from -0.1875 to 0.1875
- out_weight: bfloat16 [960, 960], P('fsdp', 'dp'), may hold values from -6 to 6
- gate_weight: bfloat16 [960, 2560], P('fsdp', 'dp'), may hold values from -0.1875 to 0.1875
- up_weight: bfloat16 [960, 2560], P('fsdp', 'dp'), may hold values from -0.1875 to 0.1875
- down_weight: bfloat16 [2560, 960], P('fsdp', 'dp'), may hold values from -0.125 to 0.125
- segment_ids: int32 [16384], P('dp'), may hold values from 0 to 2, as said below
- out_grad: bfloat16 [16384, 960], P(('dp', 'fsdp')), may hold values from -6 to 6
Outputs:
- output: bfloat16 [16384, 960], P(('dp', 'fsdp'))
- input_grad: float32 [16384, 960], P(('dp', 'fsdp'))
- gains_grad: float32 [2, 960], P(None, 'dp')
- query_grad: float32 [960, 960], P('fsdp', 'dp')
- key_grad: float32 [960, 320], P('fsdp', 'dp')
- value_grad: float32 [960, 320], P('fsdp', 'dp')
- out_weight_grad: float32 [960, 960], P('fsdp', 'dp')
- gate_grad: float32 [960, 2560], P('fsdp', 'dp')
- up_grad: float32 [960, 2560], P('fsdp', 'dp')
- down_grad: float32 [2560, 960], P('fsdp', 'dp')
The draws below stay inside these ranges and needn't reach their ends.
Inputs may be any that keep to these rules, and one draw needn't show every extreme that they name: `segment_ids`: each block of 2048 tokens (the tokens of one dp index) holds three sequences with ids 0, 1 and 2 in this order, each nonempty. Rows are counted from 0 within the block: the first row of sequence 1 lies in rows 1 to 256, and its last row lies in rows 1791 to 2046.
All inputs are finite; a program needn't handle non-finite values.
Results may differ from the reference program's by a relative error of at most 0.012.
Values may be sent and summed in bfloat16 or wider, within the bound.
No kernel may reach another device: no remote copies, remote signals or barrier semaphores. Data moves between devices by JAX's collectives and lax.ppermute only.
A program may use at most 128 MiB of HBM per device.

```python
import math
import jax
import jax.numpy as jnp
from jax import lax

D = 960
HEADS = 15
KV_HEADS = 5
HEAD_DIM = 64
FF = 2560
TOK_DEV = 512
KV_WIDTH = 320
GROUP = 2048
TOKENS = 16384


def draw_segment_ids(key, part):
    key = jax.random.fold_in(key, 7)
    start_key, end_key = jax.random.split(key, 2)
    groups = TOKENS // GROUP
    starts = jax.random.randint(start_key, (groups, 1), 1, TOK_DEV // 2 + 1)
    end_rows = GROUP - jax.random.randint(end_key, (groups, 1), 1, TOK_DEV // 2 + 1)
    row_place = jnp.arange(GROUP, dtype=jnp.int32)[None, :]
    ids = (row_place >= starts).astype(jnp.int32) + (row_place >= end_rows).astype(jnp.int32)
    return ids.reshape(TOKENS).astype(jnp.int32)


def level_of(key, shape, shards, low, high):
    loudness, own = 1.0, jax.random.fold_in(key, 6)
    for axis_at, shards_of in shards:
        draws = jnp.exp(jax.random.uniform(jax.random.fold_in(own, axis_at), (shards_of,), jnp.float32, low / len(shards), high / len(shards)))
        loudness = loudness * jnp.repeat(draws, shape[axis_at] // shards_of).reshape([-1 if axis == axis_at else 1 for axis in range(len(shape))])
    return loudness


def centred(key, shape, spread, bound, cuts=(), kind=jnp.bfloat16):
    factor_of = level_of(key, shape, cuts, -0.22, 0.18) if cuts else 1.0
    values = jax.random.normal(key, shape, jnp.float32) * spread * factor_of
    return jnp.minimum(jnp.maximum(values, -bound), bound).astype(kind)


def setup_inputs(seed: int = 0) -> dict:
    key_of = jax.random.split(jax.random.key(seed), 12)
    return {
        "tokens": centred(key_of[0], (TOKENS, D), 1.0, 6.0, ((0, 32),)),
        "norm_gains": jnp.clip(1.0 + 0.1 * jax.random.normal(key_of[1], (2, D), jnp.float32), 0.5, 1.5).astype(jnp.bfloat16),
        "query_weight": centred(key_of[2], (D, D), D ** -0.5, 0.1875, ((0, 4), (1, 8))),
        "key_weight": centred(key_of[3], (D, KV_WIDTH), D ** -0.5, 0.1875, ((0, 4), (1, 8))),
        "value_weight": centred(key_of[4], (D, KV_WIDTH), D ** -0.5, 0.1875, ((0, 4), (1, 8))),
        "out_weight": centred(key_of[5], (D, D), (max(1, 4 * D // GROUP)) ** -0.5, 6.0, ((0, 4), (1, 8))),
        "gate_weight": centred(key_of[6], (D, FF), D ** -0.5, 0.1875, ((0, 4), (1, 8))),
        "up_weight": centred(key_of[7], (D, FF), D ** -0.5, 0.1875, ((0, 4), (1, 8))),
        "down_weight": centred(key_of[8], (FF, D), FF ** -0.5, 0.125, ((0, 4), (1, 8))),
        "segment_ids": draw_segment_ids(jax.random.fold_in(key_of[11], 71), 0),
        "out_grad": centred(key_of[10], (TOKENS, D), 1.0, 6.0, ((0, 32),)),
    }


@jax.custom_vjp
def low(v):
    return lax.optimization_barrier(v.astype(jnp.bfloat16)).astype(jnp.float32)

@jax.custom_vjp
def low_back(v):
    return v

def low_keep(v):
    return (low(v), None)

def low_pass(kept, grad):
    return (grad,)

def back_keep(v):
    return (v, None)

def back_low(kept, grad):
    return (low(grad),)
low.defvjp(low_keep, low_pass)
low_back.defvjp(back_keep, back_low)
norm_eps = 1e-05
masked_value = -1e+30

def highest(operand, other):
    return jnp.dot(operand, other, precision=lax.Precision.HIGHEST)

def rms_norm(values, gain_row):
    scale_inv = lax.rsqrt(lax.optimization_barrier(jnp.mean(values * values, axis=-1, keepdims=True)) + norm_eps)
    return values * scale_inv * gain_row

def group_positions(segments):
    row_index = jnp.arange(segments.shape[0], dtype=jnp.int32)
    earlier = lax.optimization_barrier(jnp.sum((segments[None, :] < segments[:, None]).astype(jnp.int32), axis=1))
    return (row_index - earlier).astype(jnp.int32)

def rope_tables(positions):
    half_dim = HEAD_DIM // 2
    frequency = jnp.exp(jnp.arange(half_dim, dtype=jnp.float32) * (-2.0 * math.log(10000.0) / HEAD_DIM))
    angles = positions.astype(jnp.float32)[:, None] * frequency[None, :]
    return (jnp.cos(angles)[:, None, :], jnp.sin(angles)[:, None, :])

def rotate(values, cosine, sine):
    half_dim = values.shape[-1] // 2
    first_half = values[..., :half_dim]
    second = values[..., half_dim:]
    return jnp.concatenate([first_half * cosine - second * sine, second * cosine + first_half * sine], axis=-1)

def attend_group(query, keys, values, segments):
    size_rows = query.shape[0]
    row_index = jnp.arange(size_rows, dtype=jnp.int32)
    allowed = (segments[:, None] == segments[None, :]) & (row_index[None, :] <= row_index[:, None])
    ratio_heads = HEADS // KV_HEADS
    keys_heads = jnp.repeat(keys, ratio_heads, axis=1)
    values_heads = jnp.repeat(values, ratio_heads, axis=1)

    def one_head(triple):
        query_one, key_one, value_one = triple
        scores = low_back(highest(query_one, key_one.T) * 0.125)
        masked = jnp.where(allowed, scores, masked_value)
        row_max = lax.optimization_barrier(jnp.max(masked, axis=1, keepdims=True))
        log_total = row_max + jnp.log(lax.optimization_barrier(jnp.sum(jnp.exp(masked - row_max), axis=1, keepdims=True)))
        soft_probs = low(jnp.exp(masked - log_total))
        return low(low_back(highest(soft_probs, value_one)))
    heads_out = lax.map(jax.checkpoint(one_head), (query.transpose(1, 0, 2), keys_heads.transpose(1, 0, 2), values_heads.transpose(1, 0, 2)))
    return heads_out.transpose(1, 0, 2).reshape(size_rows, HEADS * HEAD_DIM)

def attention(query, keys, values, segments):
    groups = segments.shape[0] // GROUP

    def step_group(carried, pieces):
        return (carried, jax.checkpoint(attend_group)(*pieces))
    _, outputs = lax.scan(step_group, jnp.zeros((), jnp.float32), (query.reshape(groups, GROUP, HEADS, HEAD_DIM), keys.reshape(groups, GROUP, KV_HEADS, HEAD_DIM), values.reshape(groups, GROUP, KV_HEADS, HEAD_DIM), segments.reshape(groups, GROUP)))
    return outputs.reshape(groups * GROUP, HEADS * HEAD_DIM)

def forward(tokens, norm_gains, query_weight, key_weight, value_weight, out_weight, gate_weight, up_weight, down_weight, segments, cosine, sine):
    normed = low(rms_norm(tokens, norm_gains[0]))
    query = low_back(highest(normed, query_weight)).reshape(-1, HEADS, HEAD_DIM)
    keys = low_back(highest(normed, key_weight)).reshape(-1, KV_HEADS, HEAD_DIM)
    values = low(low_back(highest(normed, value_weight))).reshape(-1, KV_HEADS, HEAD_DIM)
    query = low(rotate(query, cosine, sine))
    keys = low(rotate(keys, cosine, sine))
    attended = attention(query, keys, values, segments)
    hidden = tokens + low_back(highest(attended, out_weight))
    normed_two = low(rms_norm(hidden, norm_gains[1]))
    gate_act = low_back(highest(normed_two, gate_weight))
    up_act = low_back(highest(normed_two, up_weight))
    mixed = low(gate_act * jax.nn.sigmoid(gate_act) * up_act)
    return hidden + low_back(highest(mixed, down_weight))

def reference(tokens, norm_gains, query_weight, key_weight, value_weight, out_weight, gate_weight, up_weight, down_weight, segment_ids, out_grad):
    positions = lax.map(group_positions, segment_ids.reshape(-1, GROUP)).reshape(-1)
    cosine, sine = rope_tables(positions)
    floats = (tokens.astype(jnp.float32), norm_gains.astype(jnp.float32), query_weight.astype(jnp.float32), key_weight.astype(jnp.float32), value_weight.astype(jnp.float32), out_weight.astype(jnp.float32), gate_weight.astype(jnp.float32), up_weight.astype(jnp.float32), down_weight.astype(jnp.float32))

    def closed(tokens_f, gains_f, query_f, key_f, value_f, out_f, gate_f, up_f, down_f):
        return forward(tokens_f, gains_f, query_f, key_f, value_f, out_f, gate_f, up_f, down_f, segment_ids, cosine, sine)
    output, pullback = jax.vjp(closed, *floats)
    grads = pullback(out_grad.astype(jnp.float32))
    return (output.astype(jnp.bfloat16), grads[0], grads[1], grads[2], grads[3], grads[4], grads[5], grads[6], grads[7], grads[8])
```

```python
import math

import jax
import jax.numpy as jnp
from jax import lax
from jax.experimental import pallas as pl
from jax.experimental.pallas import tpu as pltpu
from jax.sharding import PartitionSpec as P

D = 960
HEADS = 15
KV_HEADS = 5
HEAD_DIM = 64
KV_WIDTH = 320
RATIO = HEADS // KV_HEADS
HALF = HEAD_DIM // 2

norm_eps = 1e-05
masked_value = -1e30
score_scale = 0.125
score_scale_two = score_scale * math.log2(math.e)

F32 = jnp.float32
BF16 = jnp.bfloat16
FORWARD_CALLS = ((0, 5),)
BACKWARD_CALLS = ((0, 1), (1, 1), (2, 1), (3, 1), (4, 1))


def dot(a, b, contract_a, contract_b):
    return lax.dot_general(
        a, b, ((contract_a, contract_b), ((), ())), preferred_element_type=F32
    )


def strides_of(size):
    strides, stride = [], size // 2
    while stride:
        strides.append(stride)
        stride //= 2
    return strides


def swap(value, axis, size, stride):
    return lax.ppermute(value, axis, [(i, i ^ stride) for i in range(size)])


def gather_rows(values, size):
    gathered = values[None]
    for stride in strides_of(size):
        gathered = jnp.concatenate([gathered, swap(gathered, "fsdp", size, stride)], axis=0)
    return gathered


def relative_of(position, size):
    relative = 0
    for place, stride in enumerate(strides_of(size)):
        relative += ((position >> place) & 1) * stride
    return relative


def take(addend, choice):
    array, labels, fixed = addend
    fixed = {**fixed, **choice}
    starts = [fixed.get(label, 0) for label in labels] + [0, 0]
    sizes = [1 if label in fixed else 2 for label in labels] + list(array.shape[-2:])
    piece = lax.dynamic_slice(array, starts, sizes)
    return piece.reshape([n for n, label in zip(sizes, labels) if label not in fixed] + list(array.shape[-2:]))


def reduce_pieces(send, keep, order, sizes, my_bits):
    labels = [bit for bit in my_bits if bit != order[0]]
    received = swap(send, order[0][0], sizes[order[0][0]], order[0][1])
    addends = [(keep, labels, {}), (received, labels, {})]
    for bit in order[1:]:
        other = sum(take(a, {bit: 1 - my_bits[bit]}).astype(F32) for a in addends)
        received = swap(other.astype(BF16), bit[0], sizes[bit[0]], bit[1])
        addends = [(a, l, {**f, bit: my_bits[bit]}) for a, l, f in addends]
        labels = [label for label in labels if label != bit]
        addends.append((received, labels, {}))
    return sum(take(a, {}).astype(F32) for a in addends)


def place_of(relative, size):
    place = 0
    for at, stride in enumerate(strides_of(size)):
        bit = lax.rem(lax.div(relative, stride), 2)
        place = place + bit * (1 << at)
    return place


def visible(start, first_query, first_key, keys, queries):
    key_row = first_key + lax.broadcasted_iota(jnp.int32, (keys, queries), 0)
    query_row = first_query + lax.broadcasted_iota(jnp.int32, (keys, queries), 1)
    return (key_row >= start) & (key_row <= query_row)


def forward_kernel(me_ref, start_ref, q_ref, k_ref, v_ref, o_ref, lse_ref, keys, total, top, acc):
    parts, _, chunk = k_ref.shape
    rows = q_ref.shape[1]
    me = me_ref[0]
    for part in range(parts):
        keys[part] = k_ref[part].T
    start = start_ref[...]

    def block(part_at, first, later):
        at = place_of(jnp.bitwise_xor(part_at, me), parts)
        if first:
            shown = visible(start, me * rows, part_at * chunk, chunk, rows)
        else:
            shown = (part_at * chunk + lax.broadcasted_iota(jnp.int32, (chunk, rows), 0)) >= start
        for h in range(RATIO):
            head = slice(h * HEAD_DIM, (h + 1) * HEAD_DIM)
            scores = dot(keys[at], q_ref[head, :], (1,), (0,)) * score_scale_two
            scores = jnp.where(shown, scores, masked_value)
            high = jnp.max(scores, axis=0, keepdims=True)
            if not first:
                before = top[h : h + 1, :]
                high = jnp.maximum(high, before)
                shrink = jnp.exp2(before - high)
            probs = jnp.exp2(scores - high)
            sums = jnp.sum(probs, axis=0, keepdims=True)
            mixed = dot(v_ref[at], probs.astype(BF16), (1,), (0,))
            if first:
                total[h : h + 1, :] = sums
                acc[head, :] = mixed
            else:
                total[h : h + 1, :] = total[h : h + 1, :] * shrink + sums
                acc[head, :] = acc[head, :] * shrink + mixed
            top[h : h + 1, :] = high

    block(me, True, False)

    def later(part_at, carry):
        block(part_at, False, True)
        return carry

    lax.fori_loop(0, me, later, 0)
    for h in range(RATIO):
        head = slice(h * HEAD_DIM, (h + 1) * HEAD_DIM)
        sums = total[h : h + 1, :]
        o_ref[head, :] = (acc[head, :] / sums).astype(BF16)
        lse_ref[0, h : h + 1, :] = top[h : h + 1, :] + jnp.log2(sums)


def backward_kernel(
    me_ref, start_ref, cos_ref, sin_ref, q_ref, k_ref, v_ref, o_ref, do_ref, lse_ref,
    dq_ref, dk_ref, dv_ref, keys, values, acc, delta
):
    parts, _, chunk = k_ref.shape
    rows = q_ref.shape[1]
    me = me_ref[0]
    for part in range(parts):
        keys[part] = k_ref[part].T
        values[part] = v_ref[part].T
    start = start_ref[...]
    for h in range(RATIO):
        head = slice(h * HEAD_DIM, (h + 1) * HEAD_DIM)
        delta[h : h + 1, :] = jnp.sum(
            o_ref[head, :].astype(F32) * do_ref[head, :].astype(F32), axis=0, keepdims=True
        )

    def block(part_at, first):
        at = place_of(jnp.bitwise_xor(part_at, me), parts)
        if first:
            shown = visible(start, me * rows, part_at * chunk, chunk, rows)
        else:
            shown = (part_at * chunk + lax.broadcasted_iota(jnp.int32, (chunk, rows), 0)) >= start
        dk = dv = None
        for h in range(RATIO):
            head = slice(h * HEAD_DIM, (h + 1) * HEAD_DIM)
            query, grad = q_ref[head, :], do_ref[head, :]
            scores = dot(keys[at], query, (1,), (0,)) * score_scale_two
            scores = jnp.where(shown, scores, masked_value)
            probs = jnp.exp2(scores - lse_ref[0, h : h + 1, :])
            grad_probs = dot(values[at], grad, (1,), (0,))
            grad_scores = (probs * (grad_probs - delta[h : h + 1, :])).astype(BF16)
            dq = dot(k_ref[at], grad_scores, (1,), (0,))
            if first:
                acc[head, :] = dq
            else:
                acc[head, :] = acc[head, :] + dq
            dk_one = dot(query, grad_scores, (1,), (1,))
            dv_one = dot(grad, probs.astype(BF16), (1,), (1,))
            dk = dk_one if dk is None else dk + dk_one
            dv = dv_one if dv is None else dv + dv_one
        dk_ref[at] = (dk * score_scale).astype(BF16)
        dv_ref[at] = dv.astype(BF16)

    block(me, True)

    def later(part_at, carry):
        block(part_at, False)
        return carry

    lax.fori_loop(0, me, later, 0)

    def unseen(part_at, carry):
        at = place_of(jnp.bitwise_xor(part_at, me), parts)
        dk_ref[at] = jnp.zeros((HEAD_DIM, chunk), BF16)
        dv_ref[at] = jnp.zeros((HEAD_DIM, chunk), BF16)
        return carry

    lax.fori_loop(me + 1, parts, unseen, 0)
    cosine, sine = cos_ref[...], sin_ref[...]
    for h in range(RATIO):
        low = acc[h * HEAD_DIM : h * HEAD_DIM + HALF, :] * score_scale
        high = acc[h * HEAD_DIM + HALF : (h + 1) * HEAD_DIM, :] * score_scale
        dq_ref[h * HEAD_DIM : h * HEAD_DIM + HALF, :] = (low * cosine + high * sine).astype(BF16)
        dq_ref[h * HEAD_DIM + HALF : (h + 1) * HEAD_DIM, :] = (high * cosine - low * sine).astype(BF16)


def kernel_call(kernel, heads, ins, outs, scratch, cost):
    return pl.pallas_call(
        kernel,
        grid_spec=pltpu.PrefetchScalarGridSpec(
            num_scalar_prefetch=1, grid=(heads,), in_specs=ins,
            out_specs=[spec for spec, _ in outs], scratch_shapes=scratch,
        ),
        out_shape=[shape for _, shape in outs],
        cost_estimate=cost,
        compiler_params=pltpu.CompilerParams(vmem_limit_bytes=48 * 1024 * 1024),
    )


def attend_forward(me, start, query, keys_values):
    parts, _, chunk = keys_values.shape
    rows = query.shape[1]
    group = RATIO * HEAD_DIM
    attended, totals = [], []
    for first, count in FORWARD_CALLS:
        work = 2 * count * RATIO * rows * parts * chunk
        out, lse = kernel_call(
            forward_kernel,
            count,
            [
                pl.BlockSpec((1, rows), lambda g, s: (0, 0)),
                pl.BlockSpec((group, rows), lambda g, s, first=first: (g + first, 0)),
                pl.BlockSpec((parts, HEAD_DIM, chunk), lambda g, s, first=first: (0, g + first, 0)),
                pl.BlockSpec((parts, HEAD_DIM, chunk), lambda g, s, first=first: (0, KV_HEADS + g + first, 0)),
            ],
            [
                (pl.BlockSpec((group, rows), lambda g, s: (g, 0)), jax.ShapeDtypeStruct((count * group, rows), BF16)),
                (pl.BlockSpec((1, RATIO, rows), lambda g, s: (g, 0, 0)), jax.ShapeDtypeStruct((count, RATIO, rows), F32)),
            ],
            [
                pltpu.VMEM((parts, chunk, HEAD_DIM), BF16),
                pltpu.VMEM((8, rows), F32),
                pltpu.VMEM((8, rows), F32),
                pltpu.VMEM((group, rows), F32),
            ],
            pl.CostEstimate(flops=8 * HEAD_DIM * work, bytes_accessed=4_000_000, transcendentals=work // 2),
        )(me, start, query, keys_values, keys_values)
        attended.append(out)
        totals.append(lse)
    return jnp.concatenate(attended, axis=0), jnp.concatenate(totals, axis=0)


def attend_backward(me, start, cosine, sine, query, keys_values, attended, grad_attended, totals):
    parts, _, chunk = keys_values.shape
    rows = query.shape[1]
    group = RATIO * HEAD_DIM
    pieces = []
    for first, count in BACKWARD_CALLS:
        work = 2 * count * RATIO * rows * parts * chunk
        whole = lambda g, s: (0, 0)
        by_group = lambda g, s, first=first: (g + first, 0)
        pieces.append(
            kernel_call(
                backward_kernel,
                count,
                [
                    pl.BlockSpec((1, rows), whole),
                    pl.BlockSpec((HALF, rows), whole),
                    pl.BlockSpec((HALF, rows), whole),
                    pl.BlockSpec((group, rows), by_group),
                    pl.BlockSpec((parts, HEAD_DIM, chunk), lambda g, s, first=first: (0, g + first, 0)),
                    pl.BlockSpec((parts, HEAD_DIM, chunk), lambda g, s, first=first: (0, KV_HEADS + g + first, 0)),
                    pl.BlockSpec((group, rows), by_group),
                    pl.BlockSpec((group, rows), by_group),
                    pl.BlockSpec((1, RATIO, rows), lambda g, s, first=first: (g + first, 0, 0)),
                ],
                [
                    (pl.BlockSpec((group, rows), lambda g, s: (g, 0)), jax.ShapeDtypeStruct((count * group, rows), BF16)),
                    (pl.BlockSpec((parts, HEAD_DIM, chunk), lambda g, s: (0, g, 0)), jax.ShapeDtypeStruct((parts, count * HEAD_DIM, chunk), BF16)),
                    (pl.BlockSpec((parts, HEAD_DIM, chunk), lambda g, s: (0, g, 0)), jax.ShapeDtypeStruct((parts, count * HEAD_DIM, chunk), BF16)),
                ],
                [
                    pltpu.VMEM((parts, chunk, HEAD_DIM), BF16),
                    pltpu.VMEM((parts, chunk, HEAD_DIM), BF16),
                    pltpu.VMEM((group, rows), F32),
                    pltpu.VMEM((8, rows), F32),
                ],
                pl.CostEstimate(flops=20 * HEAD_DIM * work, bytes_accessed=4_000_000, transcendentals=work // 2),
            )(me, start, cosine, sine, query, keys_values, keys_values, attended, grad_attended, totals)
        )
    grad_query = jnp.concatenate([p[0] for p in pieces], axis=0)
    grad_keys_values = jnp.concatenate([p[1] for p in pieces] + [p[2] for p in pieces], axis=1)
    return grad_query, grad_keys_values


def rotate(values, cosine, sine):
    heads = values.reshape(-1, 2, HALF, values.shape[-1])
    low, high = heads[:, 0], heads[:, 1]
    return jnp.stack([low * cosine - high * sine, high * cosine + low * sine], axis=1).reshape(values.shape)


def rotate_back(values, cosine, sine):
    return rotate(values, cosine, -sine)


def make_layer(dp, fsdp):
    sizes = {"dp": dp, "fsdp": fsdp}
    dp_bits = [("dp", stride) for stride in strides_of(dp)]
    fsdp_bits = [("fsdp", stride) for stride in strides_of(fsdp)]
    near = fsdp_bits[-1]
    far = fsdp_bits[:-1]
    order_one = [near] + far[::-1] + dp_bits[::-1]
    order_two = [near] + dp_bits[::-1][:1] + far[::-1] + dp_bits[::-1][1:]

    def layer(
        tokens, norm_gains, query_weight, key_weight, value_weight, out_weight,
        gate_weight, up_weight, down_weight, segment_ids, out_grad
    ):
        rows = tokens.shape[0]
        cols = norm_gains.shape[1]
        depth = query_weight.shape[0]
        kv_cols = key_weight.shape[1]
        ff = gate_weight.shape[1] * dp
        ff_part = down_weight.shape[0]
        me = lax.axis_index("fsdp").astype(jnp.int32)
        me_dp = lax.axis_index("dp").astype(jnp.int32)
        my_bits = {bit: 0 for bit in fsdp_bits}
        my_bits.update({bit: lax.rem(lax.div(me_dp, bit[1]), 2) for bit in dp_bits})

        def gather(piece):
            return lax.all_gather(piece, ("fsdp", "dp"), axis=0, tiled=False).reshape(
                (fsdp, dp) + piece.shape
            )

        gain_row = jnp.concatenate([norm_gains[0], norm_gains[1]])
        gain_rows = jnp.pad(gain_row[None, :], ((0, 7), (0, depth - 2 * cols)))
        first = gather(jnp.concatenate([query_weight.T, key_weight.T, value_weight.T, gain_rows], axis=0))
        kv_end = cols + 2 * kv_cols
        w_query = first[:, :, :cols].reshape(fsdp, D, depth)
        w_key = first[:, :, cols : cols + kv_cols].reshape(fsdp, KV_WIDTH, depth)
        w_value = first[:, :, cols + kv_cols : kv_end].reshape(fsdp, KV_WIDTH, depth)
        gain_one = first[0, :, kv_end, :cols].reshape(1, D).astype(F32)
        gain_two = first[0, :, kv_end, cols : 2 * cols].reshape(1, D).astype(F32)
        w_out = gather(out_weight.T).reshape(fsdp, D, depth)
        w_gate = gather(gate_weight.T).reshape(fsdp, ff, depth)
        w_up = gather(up_weight.T).reshape(fsdp, ff, depth)
        w_down = gather(down_weight.T).reshape(fsdp, D, ff_part)

        ends = [jnp.sum((segment_ids < which).astype(jnp.int32)) for which in (1, 2)]
        local_ids = lax.dynamic_slice_in_dim(segment_ids, me * rows, rows)
        start = jnp.where(local_ids == 0, 0, jnp.where(local_ids == 1, ends[0], ends[1]))
        positions = me * rows + jnp.arange(rows, dtype=jnp.int32) - start
        frequency = jnp.exp(jnp.arange(HALF, dtype=F32) * (-2.0 * math.log(10000.0) / HEAD_DIM))
        angles = frequency[:, None] * positions.astype(F32)[None, :]
        cosine, sine = jnp.cos(angles), jnp.sin(angles)
        start = start[None, :]
        me_row = me[None]

        def chunks(values):
            return values.reshape(rows, fsdp, -1).transpose(1, 0, 2)

        def own_order(values):
            return [
                lax.dynamic_index_in_dim(values, jnp.bitwise_xor(me, j), 0, keepdims=False)
                for j in range(fsdp)
            ]

        inputs = tokens.astype(F32)
        inv_one = lax.rsqrt(jnp.mean(inputs * inputs, axis=1, keepdims=True) + norm_eps)
        normed = (inputs * inv_one * gain_one).astype(BF16)
        normed_parts = chunks(normed)

        def project(weight, parts):
            return dot(weight, parts, (0, 2), (0, 2))

        query = rotate(project(w_query, normed_parts), cosine, sine).astype(BF16)
        key = rotate(project(w_key, normed_parts), cosine, sine).astype(BF16)
        value = project(w_value, normed_parts).astype(BF16)
        keys_values = gather_rows(jnp.concatenate([key, value], axis=0), fsdp)
        attended, totals = attend_forward(me_row, start, query, keys_values)
        attended_parts = attended.reshape(fsdp, depth, rows)
        hidden = inputs + dot(attended_parts, w_out, (0, 1), (0, 2))
        inv_two = lax.rsqrt(jnp.mean(hidden * hidden, axis=1, keepdims=True) + norm_eps)
        normed_two = (hidden * inv_two * gain_two).astype(BF16)
        two_parts = chunks(normed_two)
        gate_act = dot(two_parts, w_gate, (0, 2), (0, 2))
        up_act = dot(two_parts, w_up, (0, 2), (0, 2))
        sigmoid = jax.nn.sigmoid(gate_act)
        mixed = (gate_act * sigmoid * up_act).astype(BF16)
        mixed_parts = chunks(mixed)
        output = hidden + dot(mixed_parts, w_down, (0, 2), (0, 2))

        def reduce(left, right_parts, order, contract=(0,), contract_right=(0,)):
            halves = []
            for wanted in (1, 0):
                terms = [
                    dot(left, part, contract, contract_right).astype(BF16)
                    for j, part in enumerate(right_parts)
                    if j % 2 == wanted
                ]
                whole = jnp.stack(terms)
                halves.append(
                    whole.reshape([2] * (len(far) + len(dp_bits)) + [-1, whole.shape[-1]])
                )
            return reduce_pieces(halves[0], halves[1], order, sizes, my_bits)

        grad_output = out_grad.astype(F32)
        sum_down = reduce(out_grad, own_order(mixed_parts), order_one)
        grad_mixed = dot(out_grad, w_down, (1,), (1,)).reshape(rows, ff)
        grad_gate = (grad_mixed * up_act * sigmoid * (1.0 + gate_act * (1.0 - sigmoid))).astype(BF16)
        grad_up = (grad_mixed * gate_act * sigmoid).astype(BF16)
        two_own = own_order(two_parts)
        sum_gate = reduce(grad_gate, two_own, order_two)
        sum_up = reduce(grad_up, two_own, order_one)
        grad_two = (dot(grad_gate, w_gate, (1,), (1,)) + dot(grad_up, w_up, (1,), (1,))).reshape(rows, D)
        weighted_two = grad_two * gain_two
        grad_gain_two = jnp.sum(grad_two * hidden * inv_two, axis=0)
        grad_hidden = (
            grad_output
            + inv_two * weighted_two
            - hidden * (inv_two * inv_two * inv_two) * jnp.mean(weighted_two * hidden, axis=1, keepdims=True)
        )
        branch_grad = grad_hidden.astype(BF16)
        sum_out = reduce(branch_grad, own_order(attended_parts), order_two, (0,), (1,))
        grad_attended = dot(w_out, branch_grad, (1,), (1,)).astype(BF16).reshape(D, rows)
        grad_query, grad_keys_values = attend_backward(
            me_row, start, cosine, sine, query, keys_values, attended, grad_attended, totals
        )
        normed_own = own_order(normed_parts)
        sum_query = reduce(grad_query, normed_own, order_two, (1,), (0,))

        mine = [grad_keys_values]
        for stride in strides_of(fsdp)[::-1]:
            half = mine[0].shape[0] // 2
            other = sum(m[half:].astype(F32) for m in mine).astype(BF16)
            mine = [m[:half] for m in mine] + [swap(other, "fsdp", fsdp, stride)]
        key_value_sum = sum(m[0].astype(F32) for m in mine)
        grad_key = rotate_back(key_value_sum[:KV_WIDTH], cosine, sine).astype(BF16)
        grad_value = key_value_sum[KV_WIDTH:].astype(BF16)
        grad_normed = (
            dot(grad_query, w_query, (0,), (1,))
            + dot(grad_key, w_key, (0,), (1,))
            + dot(grad_value, w_value, (0,), (1,))
        ).reshape(rows, D)
        weighted_one = grad_normed * gain_one
        grad_gain_one = jnp.sum(grad_normed * inputs * inv_one, axis=0)
        input_grad = (
            grad_hidden
            + inv_one * weighted_one
            - inputs * (inv_one * inv_one * inv_one) * jnp.mean(weighted_one * inputs, axis=1, keepdims=True)
        )
        both = jnp.concatenate(
            [grad_key.reshape(dp, kv_cols, rows), grad_value.reshape(dp, kv_cols, rows)], axis=1
        )
        gains_piece = jnp.concatenate(
            [grad_gain_one.reshape(dp, 1, cols), grad_gain_two.reshape(dp, 1, cols)], axis=2
        )
        gains_piece = jnp.pad(gains_piece, ((0, 0), (0, 7), (0, depth - 2 * cols))).astype(BF16)
        halves = []
        for wanted in (1, 0):
            terms = [
                jnp.concatenate(
                    [dot(both, part, (2,), (0,)).astype(BF16), gains_piece], axis=1
                )
                for j, part in enumerate(normed_own)
                if j % 2 == wanted
            ]
            whole = jnp.stack(terms)
            halves.append(whole.reshape([2] * (len(far) + len(dp_bits)) + list(whole.shape[-2:])))
        last = reduce_pieces(halves[0], halves[1], order_one, sizes, my_bits)
        return (
            output.astype(BF16),
            input_grad,
            last[2 * kv_cols, : 2 * cols].reshape(2, cols),
            sum_query.T,
            last[:kv_cols].T,
            last[kv_cols : 2 * kv_cols].T,
            sum_out.T,
            sum_gate.T,
            sum_up.T,
            sum_down.T,
        )

    return layer


def solution(mesh):
    weight = P("fsdp", "dp")
    token = P(("dp", "fsdp"), None)
    gains = P(None, "dp")
    return jax.shard_map(
        make_layer(mesh.shape["dp"], mesh.shape["fsdp"]),
        mesh=mesh,
        in_specs=(token, gains) + (weight,) * 7 + (P("dp"), token),
        out_specs=(token, token, gains) + (weight,) * 7,
        check_vma=False,
    )
```

```python
import math

import jax
import jax.numpy as jnp
from jax import lax
from jax.experimental import pallas as pl
from jax.experimental.pallas import tpu as pltpu
from jax.sharding import PartitionSpec as P

D = 960
HEADS = 15
KV_HEADS = 5
HEAD_DIM = 64
KV_WIDTH = 320
RATIO = HEADS // KV_HEADS
HALF = HEAD_DIM // 2

norm_eps = 1e-05
masked_value = -1e30
score_scale = 0.125
score_scale_two = score_scale * math.log2(math.e)

SMALL = pl.CostEstimate(flops=1_000_000, bytes_accessed=100_000, transcendentals=0)

F32 = jnp.float32
BF16 = jnp.bfloat16
FORWARD_CALLS = ((0, 1), (1, 1), (2, 1), (3, 1), (4, 1))
BACKWARD_CALLS = ((0, 1), (1, 1), (2, 1), (3, 1), (4, 1))


def dot(a, b, contract_a, contract_b):
    return lax.dot_general(
        a, b, ((contract_a, contract_b), ((), ())), preferred_element_type=F32
    )


def strides_of(size):
    strides, stride = [], size // 2
    while stride:
        strides.append(stride)
        stride //= 2
    return strides


def swap(value, bit, sizes):
    axis, stride = bit
    return lax.ppermute(value, axis, [(i, i ^ stride) for i in range(sizes[axis])])


class Chain:
    def __init__(self, steps):
        self.steps, self.result = steps, None
        self.pending = next(steps)

    def go_on(self, arrived):
        try:
            self.pending = self.steps.send(arrived)
        except StopIteration as stop:
            self.pending, self.result = None, stop.value

    def finish(self):
        while self.pending is not None:
            self.go_on(self.pending)
        return self.result


def tie(anchor, *chains):
    chains = [chain for chain in chains if chain.pending is not None]
    anchor, arrived = lax.optimization_barrier((anchor, [chain.pending for chain in chains]))
    for chain, values in zip(chains, arrived):
        chain.go_on(values)
    return anchor


def merge(own, received, bit):
    return jnp.stack([jnp.where(bit, received, own), jnp.where(bit, own, received)], axis=0)


def in_order(pieces, dp):
    count = len(strides_of(dp))
    order = list(range(count))[::-1] + [count, count + 1]
    return pieces.transpose(order).reshape(-1, pieces.shape[-1])


def take(addend, choice):
    array, labels, fixed = addend
    fixed = {**fixed, **choice}
    lanes = array.shape[-1]
    starts, sizes = [], []
    for label in labels[:-1]:
        starts.append(fixed.get(label, 0))
        sizes.append(1 if label in fixed else 2)
    at = 0
    if labels[-1] is not None and labels[-1] in fixed:
        lanes //= 2
        at = fixed[labels[-1]] * lanes
    piece = lax.dynamic_slice(array, starts + [0, at], sizes + [array.shape[-2], lanes])
    return piece.reshape([n for n in sizes if n > 1] + [array.shape[-2], lanes])


def summed(sent, kept, labels, near, order, sizes, my_bits):
    shape = [2] * (len(labels) - 1) + [-1, sent.shape[-1]]
    received = yield swap(sent, near, sizes)
    addends = [(kept.reshape(shape), labels, {}), (received.reshape(shape), labels, {})]
    for bit in order:
        other = sum(take(a, {bit: 1 - my_bits[bit]}).astype(F32) for a in addends).astype(BF16)
        received = yield swap(other, bit, sizes)
        left, lane = addends[-1][1][:-1], addends[-1][1][-1]
        left = [label for label in left if label != bit]
        addends = [(a, l, {**f, bit: my_bits[bit]}) for a, l, f in addends]
        addends.append((received, left + [None if lane == bit else lane], {}))
    return reduced(addends)


def reduced(addends):
    return sum(take(a, {}).astype(F32) for a in addends)


def place_of(relative, size):
    place = 0
    for at, stride in enumerate(strides_of(size)):
        bit = lax.rem(lax.div(relative, stride), 2)
        place = place + bit * (1 << at)
    return place


def visible(start, first_query, first_key, keys, queries):
    key_row = first_key + lax.broadcasted_iota(jnp.int32, (keys, queries), 0)
    query_row = first_query + lax.broadcasted_iota(jnp.int32, (keys, queries), 1)
    return (key_row >= start) & (key_row <= query_row)


def forward_kernel(me_ref, start_ref, q_ref, k_ref, v_ref, o_ref, lse_ref, keys, total, top, acc):
    parts, _, chunk = k_ref.shape
    rows = q_ref.shape[1]
    me = me_ref[0]
    for part in range(parts):
        keys[part] = k_ref[part].T
    start = start_ref[...]

    def block(part_at, first, later):
        at = place_of(jnp.bitwise_xor(part_at, me), parts)
        if first:
            shown = visible(start, me * rows, part_at * chunk, chunk, rows)
        else:
            shown = (part_at * chunk + lax.broadcasted_iota(jnp.int32, (chunk, rows), 0)) >= start
        for h in range(RATIO):
            head = slice(h * HEAD_DIM, (h + 1) * HEAD_DIM)
            scores = dot(keys[at], q_ref[head, :], (1,), (0,)) * score_scale_two
            scores = jnp.where(shown, scores, masked_value)
            high = jnp.max(scores, axis=0, keepdims=True)
            if not first:
                before = top[h : h + 1, :]
                high = jnp.maximum(high, before)
                shrink = jnp.exp2(before - high)
            probs = jnp.exp2(scores - high)
            sums = jnp.sum(probs, axis=0, keepdims=True)
            mixed = dot(v_ref[at], probs.astype(BF16), (1,), (0,))
            if first:
                total[h : h + 1, :] = sums
                acc[head, :] = mixed
            else:
                total[h : h + 1, :] = total[h : h + 1, :] * shrink + sums
                acc[head, :] = acc[head, :] * shrink + mixed
            top[h : h + 1, :] = high

    block(me, True, False)

    def later(part_at, carry):
        block(part_at, False, True)
        return carry

    lax.fori_loop(0, me, later, 0)
    for h in range(RATIO):
        head = slice(h * HEAD_DIM, (h + 1) * HEAD_DIM)
        sums = total[h : h + 1, :]
        o_ref[head, :] = (acc[head, :] / sums).astype(BF16)
        lse_ref[0, h : h + 1, :] = top[h : h + 1, :] + jnp.log2(sums)


def backward_kernel(
    me_ref, start_ref, cos_ref, sin_ref, q_ref, k_ref, v_ref, o_ref, do_ref, lse_ref,
    dq_ref, dk_ref, dv_ref, keys, values, acc, delta
):
    parts, _, chunk = k_ref.shape
    rows = q_ref.shape[1]
    me = me_ref[0]
    for part in range(parts):
        keys[part] = k_ref[part].T
        values[part] = v_ref[part].T
    start = start_ref[...]
    for h in range(RATIO):
        head = slice(h * HEAD_DIM, (h + 1) * HEAD_DIM)
        delta[h : h + 1, :] = jnp.sum(
            o_ref[head, :].astype(F32) * do_ref[head, :].astype(F32), axis=0, keepdims=True
        )

    def block(part_at, first):
        at = place_of(jnp.bitwise_xor(part_at, me), parts)
        if first:
            shown = visible(start, me * rows, part_at * chunk, chunk, rows)
        else:
            shown = (part_at * chunk + lax.broadcasted_iota(jnp.int32, (chunk, rows), 0)) >= start
        dk = dv = None
        for h in range(RATIO):
            head = slice(h * HEAD_DIM, (h + 1) * HEAD_DIM)
            query, grad = q_ref[head, :], do_ref[head, :]
            scores = dot(keys[at], query, (1,), (0,)) * score_scale_two
            scores = jnp.where(shown, scores, masked_value)
            probs = jnp.exp2(scores - lse_ref[0, h : h + 1, :])
            grad_probs = dot(values[at], grad, (1,), (0,))
            grad_scores = (probs * (grad_probs - delta[h : h + 1, :])).astype(BF16)
            dq = dot(k_ref[at], grad_scores, (1,), (0,))
            if first:
                acc[head, :] = dq
            else:
                acc[head, :] = acc[head, :] + dq
            dk_one = dot(query, grad_scores, (1,), (1,))
            dv_one = dot(grad, probs.astype(BF16), (1,), (1,))
            dk = dk_one if dk is None else dk + dk_one
            dv = dv_one if dv is None else dv + dv_one
        dk_ref[at] = (dk * score_scale).astype(BF16)
        dv_ref[at] = dv.astype(BF16)

    block(me, True)

    def later(part_at, carry):
        block(part_at, False)
        return carry

    lax.fori_loop(0, me, later, 0)

    def unseen(part_at, carry):
        at = place_of(jnp.bitwise_xor(part_at, me), parts)
        dk_ref[at] = jnp.zeros((HEAD_DIM, chunk), BF16)
        dv_ref[at] = jnp.zeros((HEAD_DIM, chunk), BF16)
        return carry

    lax.fori_loop(me + 1, parts, unseen, 0)
    cosine, sine = cos_ref[...], sin_ref[...]
    for h in range(RATIO):
        low = acc[h * HEAD_DIM : h * HEAD_DIM + HALF, :] * score_scale
        high = acc[h * HEAD_DIM + HALF : (h + 1) * HEAD_DIM, :] * score_scale
        dq_ref[h * HEAD_DIM : h * HEAD_DIM + HALF, :] = (low * cosine + high * sine).astype(BF16)
        dq_ref[h * HEAD_DIM + HALF : (h + 1) * HEAD_DIM, :] = (high * cosine - low * sine).astype(BF16)


def kernel_call(kernel, heads, ins, outs, scratch, cost):
    return pl.pallas_call(
        kernel,
        grid_spec=pltpu.PrefetchScalarGridSpec(
            num_scalar_prefetch=1, grid=(heads,), in_specs=ins,
            out_specs=[spec for spec, _ in outs], scratch_shapes=scratch,
        ),
        out_shape=[shape for _, shape in outs],
        cost_estimate=cost,
        compiler_params=pltpu.CompilerParams(vmem_limit_bytes=48 * 1024 * 1024),
    )


def attend_forward(me, start, query, keys_values, ties):
    parts, _, chunk = keys_values.shape
    rows = query.shape[1]
    group = RATIO * HEAD_DIM
    attended, totals = [], []
    for first, count in FORWARD_CALLS:
        if attended:
            me, attended[-1] = tie((me, attended[-1]), *ties[first])
        out, lse = kernel_call(
            forward_kernel,
            count,
            [
                pl.BlockSpec((1, rows), lambda g, s: (0, 0)),
                pl.BlockSpec((group, rows), lambda g, s, first=first: (g + first, 0)),
                pl.BlockSpec((parts, HEAD_DIM, chunk), lambda g, s, first=first: (0, g + first, 0)),
                pl.BlockSpec((parts, HEAD_DIM, chunk), lambda g, s, first=first: (0, KV_HEADS + g + first, 0)),
            ],
            [
                (pl.BlockSpec((group, rows), lambda g, s: (g, 0)), jax.ShapeDtypeStruct((count * group, rows), BF16)),
                (pl.BlockSpec((1, RATIO, rows), lambda g, s: (g, 0, 0)), jax.ShapeDtypeStruct((count, RATIO, rows), F32)),
            ],
            [
                pltpu.VMEM((parts, chunk, HEAD_DIM), BF16),
                pltpu.VMEM((8, rows), F32),
                pltpu.VMEM((8, rows), F32),
                pltpu.VMEM((group, rows), F32),
            ],
            SMALL,
        )(me, start, query, keys_values, keys_values)
        attended.append(out)
        totals.append(lse)
    return jnp.concatenate(attended, axis=0), jnp.concatenate(totals, axis=0)


def attend_backward(me, start, cosine, sine, query, keys_values, attended, grad_attended, totals, ties):
    parts, _, chunk = keys_values.shape
    rows = query.shape[1]
    group = RATIO * HEAD_DIM
    pieces = []
    for first, count in BACKWARD_CALLS:
        if pieces:
            me, pieces[-1] = tie((me, pieces[-1]), *ties[first])
        else:
            me = tie(me, *ties[first])
        whole = lambda g, s: (0, 0)
        by_group = lambda g, s, first=first: (g + first, 0)
        pieces.append(
            kernel_call(
                backward_kernel,
                count,
                [
                    pl.BlockSpec((1, rows), whole),
                    pl.BlockSpec((HALF, rows), whole),
                    pl.BlockSpec((HALF, rows), whole),
                    pl.BlockSpec((group, rows), by_group),
                    pl.BlockSpec((parts, HEAD_DIM, chunk), lambda g, s, first=first: (0, g + first, 0)),
                    pl.BlockSpec((parts, HEAD_DIM, chunk), lambda g, s, first=first: (0, KV_HEADS + g + first, 0)),
                    pl.BlockSpec((group, rows), by_group),
                    pl.BlockSpec((group, rows), by_group),
                    pl.BlockSpec((1, RATIO, rows), lambda g, s, first=first: (g + first, 0, 0)),
                ],
                [
                    (pl.BlockSpec((group, rows), lambda g, s: (g, 0)), jax.ShapeDtypeStruct((count * group, rows), BF16)),
                    (pl.BlockSpec((parts, HEAD_DIM, chunk), lambda g, s: (0, g, 0)), jax.ShapeDtypeStruct((parts, count * HEAD_DIM, chunk), BF16)),
                    (pl.BlockSpec((parts, HEAD_DIM, chunk), lambda g, s: (0, g, 0)), jax.ShapeDtypeStruct((parts, count * HEAD_DIM, chunk), BF16)),
                ],
                [
                    pltpu.VMEM((parts, chunk, HEAD_DIM), BF16),
                    pltpu.VMEM((parts, chunk, HEAD_DIM), BF16),
                    pltpu.VMEM((group, rows), F32),
                    pltpu.VMEM((8, rows), F32),
                ],
                SMALL,
            )(me, start, cosine, sine, query, keys_values, keys_values, attended, grad_attended, totals)
        )
    grad_query = jnp.concatenate([p[0] for p in pieces], axis=0)
    grad_keys_values = jnp.concatenate([p[1] for p in pieces] + [p[2] for p in pieces], axis=1)
    return grad_query, grad_keys_values


def feed_kernel(me_ref, x_ref, o_ref, gain_ref, dy_ref, grad_ref, *refs):
    outs, gates, ups, downs = refs[0:4], refs[4:8], refs[8:12], refs[12:16]
    (
        y_ref, h_ref, m_ref, dg_ref, du_ref, n_ref, dh_ref, dz_ref, do_ref, sums_ref,
        dx_ref, down, arrived
    ) = refs[16:]
    at = pl.program_id(0)
    me = me_ref[0]
    tile = 256
    tiles = x_ref.shape[1] // tile
    width = y_ref.shape[1]
    depth = do_ref.shape[1]

    def bring(j):
        return pltpu.make_async_copy(downs[j], down.at[j % 2], arrived.at[j % 2])

    for j in range(4):
        @pl.when(at == j)
        def _():
            if j == 0:
                bring(0).start()
            bring(j).wait()
            if j < 3:
                bring(j + 1).start()

    here = down.at[lax.rem(at, 2)]

    def rows_of(row):
        return pl.ds(pl.multiple_of(row * tile, tile), tile)

    def scale_of(hidden):
        mean = sum(jnp.sum(h * h, axis=1, keepdims=True) for h in hidden) * (1.0 / width)
        return lax.rsqrt(mean + norm_eps)

    def piece(ref):
        return ref[...].reshape(-1, ref.shape[-1])

    def before(row, carry):
        rows = rows_of(row)
        heads = [o_ref[jnp.bitwise_xor(me, k), :, rows].T for k in range(4)]
        hidden = []
        for j in range(4):
            h = x_ref[j, rows, :].astype(F32)
            for k in range(4):
                h = h + dot(heads[k], outs[k][jnp.bitwise_xor(me, j)], (1,), (1,))
            h_ref[jnp.bitwise_xor(me, j), rows, :] = h
            hidden.append(h)
        scale = scale_of(hidden)
        for j in range(4):
            n_ref[j, rows, :] = (hidden[j] * scale * gain_ref[j]).astype(BF16)
        return carry

    @pl.when(at == 0)
    def _():
        lax.fori_loop(0, tiles, before, 0)

    def some_rows(row, carry):
        rows = rows_of(row)
        gate = sum(dot(n_ref[k, rows, :], piece(gates[k]), (1,), (1,)) for k in range(4))
        up = sum(dot(n_ref[k, rows, :], piece(ups[k]), (1,), (1,)) for k in range(4))
        sigmoid = jax.nn.sigmoid(gate)
        mixed = (gate * sigmoid * up).astype(BF16)
        m_ref[0, rows, :] = mixed
        y = dot(mixed, here[...], (1,), (1,))
        grad_mixed = dot(dy_ref[rows, :], here[...], (1,), (0,))
        grad_gate = (grad_mixed * up * sigmoid * (1.0 + gate * (1.0 - sigmoid))).astype(BF16)
        grad_up = (grad_mixed * gate * sigmoid).astype(BF16)
        dg_ref[rows, :] = grad_gate
        du_ref[rows, :] = grad_up
        dx = [
            dot(grad_gate, piece(gates[k]), (1,), (0,)) + dot(grad_up, piece(ups[k]), (1,), (0,))
            for k in range(4)
        ]

        @pl.when(at == 0)
        def _():
            y_ref[rows, :] = y
            for k in range(4):
                dx_ref[k, rows, :] = dx[k]

        @pl.when(at > 0)
        def _():
            y_ref[rows, :] = y_ref[rows, :] + y
            for k in range(4):
                dx_ref[k, rows, :] = dx_ref[k, rows, :] + dx[k]

        return carry

    lax.fori_loop(0, tiles, some_rows, 0)

    def behind(row, carry):
        rows = rows_of(row)
        hidden = [h_ref[jnp.bitwise_xor(me, j), rows, :] for j in range(4)]
        scale = scale_of(hidden)
        grads = [dx_ref[j, rows, :] for j in range(4)]
        weighted = [grads[j] * gain_ref[j] for j in range(4)]
        mean = sum(
            jnp.sum(weighted[j] * hidden[j], axis=1, keepdims=True) for j in range(4)
        ) * (1.0 / width)
        cubed = scale * scale * scale * mean
        low = []
        for j in range(4):
            place = jnp.bitwise_xor(me, j)
            sums_ref[place] = sums_ref[place] + jnp.sum(grads[j] * hidden[j] * scale, axis=0, keepdims=True)
            dh = grad_ref[j, rows, :].astype(F32) + scale * weighted[j] - hidden[j] * cubed
            dh_ref[place, rows, :] = dh
            low.append(dh.astype(BF16))
            dz_ref[place, rows, :] = low[j]
        for k in range(4):
            do = sum(dot(low[j], outs[k][jnp.bitwise_xor(me, j)], (1,), (0,)) for j in range(4))
            do_ref[jnp.bitwise_xor(me, k), :, rows] = do.astype(BF16).T[:depth]
        return carry

    @pl.when(at == 3)
    def _():
        sums_ref[...] = jnp.zeros_like(sums_ref)
        lax.fori_loop(0, tiles, behind, 0)


def feed_forward(me, tokens, attended, gain, grad, grad_chunks, outs, gates, ups, downs):
    rows, width = grad.shape
    low, _, _, height, lanes = gates[0].shape
    part = downs[0].shape[1]
    ff = 4 * part
    depth = width // 4

    def held(shape):
        return pl.BlockSpec(shape, lambda j, s: (0,) * len(shape))

    def high_bits(j, s):
        chunk = jnp.bitwise_xor(s[0], j)
        return lax.div(chunk, 2), lax.rem(chunk, 2)

    def gate_place(j, s):
        highest, second = high_bits(j, s)
        return 0, second, highest, 0, 0

    def up_place(j, s):
        highest, second = high_bits(j, s)
        return second, 0, highest, 0, 0

    gate_block = pl.BlockSpec((low, 1, 1, height, lanes), gate_place)
    up_block = pl.BlockSpec((1, low, 1, height, lanes), up_place)
    wide_block = pl.BlockSpec((rows, part), lambda j, s: (0, jnp.bitwise_xor(s[0], j)))
    wide = jax.ShapeDtypeStruct((rows, ff), BF16)
    chunked = (4, rows, lanes)
    return pl.pallas_call(
        feed_kernel,
        grid_spec=pltpu.PrefetchScalarGridSpec(
            num_scalar_prefetch=1,
            grid=(4,),
            in_specs=[held(chunked), held(attended.shape), held(gain.shape), held(grad.shape), held(chunked)]
            + [held(outs[0].shape)] * 4
            + [gate_block] * 4
            + [up_block] * 4
            + [pl.BlockSpec(memory_space=pl.ANY)] * 4,
            out_specs=[
                held(grad.shape), held(chunked), pl.BlockSpec((1, rows, part), lambda j, s: (j, 0, 0)),
                wide_block, wide_block, held(chunked), held(chunked), held(chunked),
                held((4, depth, rows)), held((4, 1, lanes)),
            ],
            scratch_shapes=[
                pltpu.VMEM(chunked, F32), pltpu.VMEM((2,) + downs[0].shape, BF16), pltpu.SemaphoreType.DMA((2,))
            ],
        ),
        out_shape=[
            jax.ShapeDtypeStruct((rows, width), F32), jax.ShapeDtypeStruct(chunked, F32),
            jax.ShapeDtypeStruct((4, rows, part), BF16), wide, wide,
            jax.ShapeDtypeStruct(chunked, BF16), jax.ShapeDtypeStruct(chunked, F32),
            jax.ShapeDtypeStruct(chunked, BF16), jax.ShapeDtypeStruct((4, depth, rows), BF16),
            jax.ShapeDtypeStruct((4, 1, lanes), F32),
        ],
        cost_estimate=pl.CostEstimate(flops=12 * rows * width * ff, bytes_accessed=40_000_000, transcendentals=rows * ff),
        compiler_params=pltpu.CompilerParams(vmem_limit_bytes=58 * 1024 * 1024),
    )(me, tokens, attended, gain, grad, grad_chunks, *outs, *gates, *ups, *downs)


def rotate(values, cosine, sine):
    heads = values.reshape(-1, 2, HALF, values.shape[-1])
    low, high = heads[:, 0], heads[:, 1]
    return jnp.stack([low * cosine - high * sine, high * cosine + low * sine], axis=1).reshape(values.shape)


def rotate_back(values, cosine, sine):
    return rotate(values, cosine, -sine)


def make_layer(dp, fsdp):
    sizes = {"dp": dp, "fsdp": fsdp}
    dp_bits = [("dp", stride) for stride in strides_of(dp)]
    far, near = [("fsdp", stride) for stride in strides_of(fsdp)]
    order_one = [far] + dp_bits[::-1]
    order_two = [dp_bits[-1], far] + dp_bits[:-1][::-1]
    order_three = [dp_bits[1], far] + dp_bits[2:][::-1] + dp_bits[:1]

    def layer(
        tokens, norm_gains, query_weight, key_weight, value_weight, out_weight,
        gate_weight, up_weight, down_weight, segment_ids, out_grad
    ):
        rows = tokens.shape[0]
        cols = norm_gains.shape[1]
        depth = query_weight.shape[0]
        lanes = -(-depth // 128) * 128
        kv_cols = key_weight.shape[1]
        ff = gate_weight.shape[1] * dp
        me = lax.axis_index("fsdp").astype(jnp.int32)
        me_dp = lax.axis_index("dp").astype(jnp.int32)
        my_bits = {far: 0, near: 0}
        my_bits.update({bit: lax.rem(lax.div(me_dp, bit[1]), 2) for bit in dp_bits})


        def fill(piece):
            return jnp.pad(piece, ((0, 0), (0, -piece.shape[1] % 128)))

        def add_bits(piece, bits):
            for bit in bits:
                arrived = yield swap(piece, bit, sizes)
                piece = merge(piece, arrived, my_bits[bit] == 1)
            return piece

        def first_bits(piece):
            return add_bits(piece, dp_bits[:-1])

        last = dp_bits[-1]

        def with_last(piece, arrived):
            return merge(piece, arrived, my_bits[last] == 1)

        def spread_one(piece):
            arrived = yield swap(piece, last, sizes)
            own = with_last(piece, arrived)
            far_one, near_one = yield (swap(own, far, sizes), swap(own, near, sizes))
            both = yield swap(far_one, near, sizes)
            return [own, near_one, far_one, both]

        def spread_two(piece):
            other, side = yield (swap(piece, far, sizes), swap(piece, last, sizes))
            own = with_last(piece, side)
            other_side, near_one = yield (swap(other, last, sizes), swap(own, near, sizes))
            far_one = with_last(other, other_side)
            both = yield swap(far_one, near, sizes)
            return [own, near_one, far_one, both]

        def spread_two_late(piece):
            side = yield swap(piece, last, sizes)
            own = with_last(piece, side)
            other, near_one = yield (swap(piece, far, sizes), swap(own, near, sizes))
            other_side = yield swap(other, last, sizes)
            far_one = with_last(other, other_side)
            both = yield swap(far_one, near, sizes)
            return [own, near_one, far_one, both]

        def spread_three(piece):
            own = yield from add_bits(piece, dp_bits[2:])
            other = yield swap(own, far, sizes)
            bit = dp_bits[1]
            sides = yield (swap(own, bit, sizes), swap(other, bit, sizes))
            own, far_one = [merge(p, s, my_bits[bit] == 1) for p, s in zip((own, other), sides)]
            near_one, both = yield (swap(own, near, sizes), swap(far_one, near, sizes))
            return [own, near_one, far_one, both]

        def whole_way(piece, bits, steps):
            piece = yield from add_bits(piece, bits)
            return (yield from steps(piece))

        gain_row = jnp.concatenate([norm_gains[0], norm_gains[1]])
        gain_rows = jnp.pad(gain_row[None, :], ((0, 7), (0, depth - 2 * cols)))
        kv_end = 2 * kv_cols
        own_first = fill(jnp.concatenate([query_weight.T, key_weight.T, value_weight.T, gain_rows], axis=0))
        own_second = fill(jnp.concatenate([gate_weight.T, up_weight.T], axis=0))
        own_out, own_down = fill(out_weight.T), fill(down_weight.T)

        first_chain = Chain(first_bits(own_first))
        second_chain = Chain(add_bits(own_second, dp_bits[:1]))
        while first_chain.pending is not None:
            first_chain.go_on(first_chain.pending)
            if first_chain.pending is not None:
                tie((), first_chain, second_chain)
        first = first_chain.finish()
        second = second_chain.finish()
        half = gate_weight.shape[1]
        gate_chain = Chain(whole_way(second[..., :half, :], dp_bits[1:-1], spread_two_late))
        up_chain = Chain(spread_three(second[..., half:, :]))
        own_out, own_down, first = lax.optimization_barrier((own_out, own_down, first))
        out_chain = Chain(whole_way(own_out, dp_bits[:-1], spread_one))
        down_chain = Chain(whole_way(own_down, dp_bits[:-1], spread_two))
        query_chain = Chain(spread_one(first[..., :cols, :]))
        rest_chain = Chain(spread_two(first[..., cols:, :]))
        rest = rest_chain.finish()
        rest_rows = [in_order(r, dp).reshape(dp, -1, lanes) for r in rest]
        w_key = [r[:, :kv_cols].reshape(KV_WIDTH, lanes) for r in rest_rows]
        w_value = [r[:, kv_cols:kv_end].reshape(KV_WIDTH, lanes) for r in rest_rows]
        gain_one = rest_rows[0][:, kv_end, :cols].reshape(1, D).astype(F32)
        gain_two = rest_rows[0][:, kv_end, cols : 2 * cols].reshape(1, D).astype(F32)
        w_query = [in_order(w, dp) for w in query_chain.finish()]

        ends = [jnp.sum((segment_ids < which).astype(jnp.int32)) for which in (1, 2)]
        local_ids = lax.dynamic_slice_in_dim(segment_ids, me * rows, rows)
        start = jnp.where(local_ids == 0, 0, jnp.where(local_ids == 1, ends[0], ends[1]))
        positions = me * rows + jnp.arange(rows, dtype=jnp.int32) - start
        frequency = jnp.exp(jnp.arange(HALF, dtype=F32) * (-2.0 * math.log(10000.0) / HEAD_DIM))
        angles = frequency[:, None] * positions.astype(F32)[None, :]
        cosine, sine = jnp.cos(angles), jnp.sin(angles)
        start = start[None, :]
        me_row = me[None]

        def pick(values, j):
            return lax.dynamic_index_in_dim(values, jnp.bitwise_xor(me, j), 0, keepdims=False)

        def relative_chunks(values):
            parts = values.reshape(rows, fsdp, -1).transpose(1, 0, 2)
            parts = jnp.pad(parts, ((0, 0), (0, 0), (0, -parts.shape[2] % 128)))
            return jnp.stack([pick(parts, j) for j in range(fsdp)])

        def columns_of(chunks):
            return jnp.concatenate([pick(chunks, f)[:, :depth] for f in range(fsdp)], axis=1)

        inputs = tokens.astype(F32)
        inv_one = lax.rsqrt(jnp.mean(inputs * inputs, axis=1, keepdims=True) + norm_eps)
        normed = (inputs * inv_one * gain_one).astype(BF16)
        normed_parts = relative_chunks(normed)

        def project(weight, parts):
            return sum(dot(weight[j], parts[j], (1,), (1,)) for j in range(fsdp))

        key = rotate(project(w_key, normed_parts), cosine, sine).astype(BF16)
        value = project(w_value, normed_parts).astype(BF16)
        normed_parts = tie(normed_parts, gate_chain, up_chain, out_chain, down_chain)
        query = rotate(project(w_query, normed_parts), cosine, sine).astype(BF16)
        pair = jnp.concatenate([key, value], axis=0)[None]
        far_pair = swap(pair, far, sizes)
        far_pair = tie(far_pair, gate_chain, up_chain, out_chain, down_chain)
        pair = jnp.concatenate([pair, far_pair], axis=0)
        keys_values = jnp.concatenate([pair, swap(pair, near, sizes)], axis=0)
        attended, totals = attend_forward(
            me_row,
            start,
            query,
            keys_values,
            [[], [out_chain], [gate_chain], [down_chain, up_chain], [gate_chain, out_chain]],
        )
        filled = ((0, 0), (0, lanes - depth), (0, 0))
        attended_parts = jnp.pad(attended.reshape(fsdp, depth, rows), filled)
        w_out = [
            jnp.pad(in_order(w, dp).reshape(fsdp, depth, lanes), filled) for w in out_chain.finish()
        ]

        def low_bits(pieces, first):
            low = len(dp_bits) - 2
            order = list(range(pieces.ndim))
            order[first : first + low] = order[first : first + low][::-1]
            shape = list(pieces.shape)
            shape[first : first + low] = [dp // 4]
            return pieces.transpose(order).reshape(shape)

        w_gate = [low_bits(w, 0) for w in gate_chain.finish()]
        w_up = [low_bits(w, 1) for w in up_chain.finish()]
        w_down = [in_order(w, dp) for w in down_chain.finish()]

        attended_own = jnp.stack([pick(attended_parts, j) for j in range(fsdp)])
        gain_own = relative_chunks(jnp.broadcast_to(gain_two, (rows, D)))[:, :1]
        fed, hidden, mixed, grad_gate, grad_up, two_own, grad_hidden, branch_grad, grad_attended, gain_sums = (
            feed_forward(
                me_row, relative_chunks(tokens), attended_parts, gain_own, out_grad,
                relative_chunks(out_grad), w_out, w_gate, w_up, w_down
            )
        )
        grad_attended = grad_attended.reshape(D, rows)


        def halves_of(right_own):
            return [jnp.concatenate([right_own[w], right_own[w + 2]], axis=1) for w in (1, 0)]

        def start_sum(sent, kept, order):
            return Chain(summed(sent, kept, dp_bits + [far], near, order, sizes, my_bits))

        def product_sum(left, right_own, order, contract=(0,)):
            sent, kept = [dot(left, r, contract, (0,)).astype(BF16) for r in halves_of(right_own)]
            return start_sum(sent, kept, order)

        sum_down = product_sum(out_grad, mixed, order_one)
        sum_gate = product_sum(grad_gate, two_own, order_two)
        sum_up = product_sum(grad_up, two_own, order_three)
        def out_product(right):
            whole = lax.dot_general(
                branch_grad, right, (((1,), (0,)), ((), ())), preferred_element_type=F32
            )
            return whole[:, :depth].astype(BF16).reshape(D, right.shape[1])

        sum_out = start_sum(
            *[out_product(r) for r in halves_of(attended_own.transpose(0, 2, 1))], order_two
        )

        early = [sum_down, sum_gate, sum_up, sum_out]
        grad_query, grad_keys_values = attend_backward(
            me_row, start, cosine, sine, query, keys_values, attended, grad_attended, totals,
            [early, [], early, [], [sum_down]],
        )
        sum_query = product_sum(grad_query, normed_parts, order_two, (1,))

        near_kv = swap(grad_keys_values[2:], near, sizes)
        near_kv, hidden, fed, grad_hidden, gain_sums = tie(
            (near_kv, hidden, fed, grad_hidden, gain_sums), sum_query, sum_up
        )
        far_kv = swap(
            (grad_keys_values[1].astype(F32) + near_kv[1].astype(F32)).astype(BF16), far, sizes
        )
        far_kv = tie(far_kv, sum_query, sum_gate, sum_out, sum_down, sum_up)

        def plain(chunks):
            return jnp.concatenate([chunks[f][:, :depth] for f in range(fsdp)], axis=1)

        output = plain(hidden) + fed
        grad_hidden = plain(grad_hidden)
        grad_gain_two = plain(gain_sums).reshape(D)
        key_value_sum = (
            grad_keys_values[0].astype(F32) + near_kv[0].astype(F32) + far_kv.astype(F32)
        )
        grad_key = rotate_back(key_value_sum[:KV_WIDTH], cosine, sine).astype(BF16)
        grad_value = key_value_sum[KV_WIDTH:].astype(BF16)
        grad_normed = columns_of(
            jnp.stack(
                [
                    dot(grad_query, w_query[j], (0,), (0,))
                    + dot(grad_key, w_key[j], (0,), (0,))
                    + dot(grad_value, w_value[j], (0,), (0,))
                    for j in range(fsdp)
                ]
            )
        )
        weighted_one = grad_normed * gain_one
        grad_gain_one = jnp.sum(grad_normed * inputs * inv_one, axis=0)
        input_grad = (
            grad_hidden
            + inv_one * weighted_one
            - inputs * (inv_one * inv_one * inv_one) * jnp.mean(weighted_one * inputs, axis=1, keepdims=True)
        )
        both = jnp.concatenate(
            [grad_key.reshape(dp, kv_cols, rows), grad_value.reshape(dp, kv_cols, rows)], axis=1
        ).reshape(dp * kv_end, rows)
        gains_piece = jnp.concatenate(
            [grad_gain_one.reshape(dp, 1, cols), grad_gain_two.reshape(dp, 1, cols)], axis=2
        )
        gains_piece = fill(
            jnp.pad(gains_piece, ((0, 0), (0, 7), (0, 0))).reshape(dp * 8, 2 * cols)
        ).astype(BF16)
        gains_piece = jnp.pad(gains_piece, ((0, 0), (0, lanes - gains_piece.shape[1]))).reshape(dp, 8, lanes)
        gains_piece = jnp.concatenate([gains_piece, gains_piece], axis=2)
        sent, kept = [
            jnp.concatenate([dot(both, r, (1,), (0,)).astype(BF16).reshape(dp, kv_end, 2 * lanes), gains_piece], axis=1)
            for r in halves_of(normed_parts)
        ]
        last_sum = start_sum(sent, kept, order_one).finish()
        out_down, out_gate, out_up, out_out, out_query = [
            chain.finish() for chain in (sum_down, sum_gate, sum_up, sum_out, sum_query)
        ]
        return (
            output.astype(BF16),
            input_grad,
            last_sum[kv_end, : 2 * cols].reshape(2, cols),
            out_query[:, :depth].T,
            last_sum[:kv_cols, :depth].T,
            last_sum[kv_cols:kv_end, :depth].T,
            out_out[:, :depth].T,
            out_gate[:, :depth].T,
            out_up[:, :depth].T,
            out_down.T,
        )

    return layer


def solution(mesh):
    weight = P("fsdp", "dp")
    token = P(("dp", "fsdp"), None)
    gains = P(None, "dp")
    return jax.shard_map(
        make_layer(mesh.shape["dp"], mesh.shape["fsdp"]),
        mesh=mesh,
        in_specs=(token, gains) + (weight,) * 7 + (P("dp"), token),
        out_specs=(token, token, gains) + (weight,) * 7,
        check_vma=False,
    )
```

```python
import math

import jax
import jax.numpy as jnp
from jax import lax
from jax.experimental import pallas as pl
from jax.experimental.pallas import tpu as pltpu
from jax.sharding import PartitionSpec as P

D = 960
HEADS = 15
KV_HEADS = 5
HEAD_DIM = 64
KV_WIDTH = 320
RATIO = HEADS // KV_HEADS
HALF = HEAD_DIM // 2

norm_eps = 1e-05
masked_value = -1e30
score_scale = 0.125
score_scale_two = score_scale * math.log2(math.e)

SMALL = pl.CostEstimate(flops=1_000_000, bytes_accessed=100_000, transcendentals=0)

F32 = jnp.float32
BF16 = jnp.bfloat16
FORWARD_CALLS = ((0, 1), (1, 1), (2, 1), (3, 1), (4, 1))
BACKWARD_CALLS = ((0, 1), (1, 1), (2, 1), (3, 1), (4, 1))


def dot(a, b, contract_a, contract_b):
    return lax.dot_general(
        a, b, ((contract_a, contract_b), ((), ())), preferred_element_type=F32
    )


def strides_of(size):
    strides, stride = [], size // 2
    while stride:
        strides.append(stride)
        stride //= 2
    return strides


def swap(value, bit, sizes):
    axis, stride = bit
    return lax.ppermute(value, axis, [(i, i ^ stride) for i in range(sizes[axis])])


class Chain:
    def __init__(self, steps):
        self.steps, self.result = steps, None
        self.pending = next(steps)

    def go_on(self, arrived):
        try:
            self.pending = self.steps.send(arrived)
        except StopIteration as stop:
            self.pending, self.result = None, stop.value

    def finish(self):
        while self.pending is not None:
            self.go_on(self.pending)
        return self.result


def tie(anchor, *chains):
    chains = [chain for chain in chains if chain.pending is not None]
    anchor, arrived = lax.optimization_barrier((anchor, [chain.pending for chain in chains]))
    for chain, values in zip(chains, arrived):
        chain.go_on(values)
    return anchor


def merge(own, received, bit):
    return jnp.stack([jnp.where(bit, received, own), jnp.where(bit, own, received)], axis=0)


def in_order(pieces, dp):
    count = len(strides_of(dp))
    order = list(range(count))[::-1] + [count, count + 1]
    return pieces.transpose(order).reshape(-1, pieces.shape[-1])


def take(addend, choice):
    array, labels, fixed = addend
    fixed = {**fixed, **choice}
    lanes = array.shape[-1]
    starts, sizes = [], []
    for label in labels[:-1]:
        starts.append(fixed.get(label, 0))
        sizes.append(1 if label in fixed else 2)
    at = 0
    if labels[-1] is not None and labels[-1] in fixed:
        lanes //= 2
        at = fixed[labels[-1]] * lanes
    piece = lax.dynamic_slice(array, starts + [0, at], sizes + [array.shape[-2], lanes])
    return piece.reshape([n for n in sizes if n > 1] + [array.shape[-2], lanes])


def summed(sent, kept, labels, near, order, sizes, my_bits):
    shape = [2] * (len(labels) - 1) + [-1, sent.shape[-1]]
    received = yield swap(sent, near, sizes)
    addends = [(kept.reshape(shape), labels, {}), (received.reshape(shape), labels, {})]
    for bit in order:
        other = sum(take(a, {bit: 1 - my_bits[bit]}).astype(F32) for a in addends).astype(BF16)
        received = yield swap(other, bit, sizes)
        left, lane = addends[-1][1][:-1], addends[-1][1][-1]
        left = [label for label in left if label != bit]
        addends = [(a, l, {**f, bit: my_bits[bit]}) for a, l, f in addends]
        addends.append((received, left + [None if lane == bit else lane], {}))
    return reduced(addends)


def reduced(addends):
    return sum(take(a, {}).astype(F32) for a in addends)


def place_of(relative, size):
    place = 0
    for at, stride in enumerate(strides_of(size)):
        bit = lax.rem(lax.div(relative, stride), 2)
        place = place + bit * (1 << at)
    return place


def visible(start, first_query, first_key, keys, queries):
    key_row = first_key + lax.broadcasted_iota(jnp.int32, (keys, queries), 0)
    query_row = first_query + lax.broadcasted_iota(jnp.int32, (keys, queries), 1)
    return (key_row >= start) & (key_row <= query_row)


def forward_kernel(me_ref, start_ref, q_ref, k_ref, v_ref, o_ref, lse_ref, keys, total, top, acc):
    parts, _, chunk = k_ref.shape
    rows = q_ref.shape[1]
    me = me_ref[0]
    for part in range(parts):
        keys[part] = k_ref[part].T
    start = start_ref[...]

    def block(part_at, first, later):
        at = place_of(jnp.bitwise_xor(part_at, me), parts)
        if first:
            shown = visible(start, me * rows, part_at * chunk, chunk, rows)
        else:
            shown = (part_at * chunk + lax.broadcasted_iota(jnp.int32, (chunk, rows), 0)) >= start
        for h in range(RATIO):
            head = slice(h * HEAD_DIM, (h + 1) * HEAD_DIM)
            scores = dot(keys[at], q_ref[head, :], (1,), (0,)) * score_scale_two
            scores = jnp.where(shown, scores, masked_value)
            high = jnp.max(scores, axis=0, keepdims=True)
            if not first:
                before = top[h : h + 1, :]
                high = jnp.maximum(high, before)
                shrink = jnp.exp2(before - high)
            probs = jnp.exp2(scores - high)
            sums = jnp.sum(probs, axis=0, keepdims=True)
            mixed = dot(v_ref[at], probs.astype(BF16), (1,), (0,))
            if first:
                total[h : h + 1, :] = sums
                acc[head, :] = mixed
            else:
                total[h : h + 1, :] = total[h : h + 1, :] * shrink + sums
                acc[head, :] = acc[head, :] * shrink + mixed
            top[h : h + 1, :] = high

    block(me, True, False)

    def later(part_at, carry):
        block(part_at, False, True)
        return carry

    lax.fori_loop(0, me, later, 0)
    for h in range(RATIO):
        head = slice(h * HEAD_DIM, (h + 1) * HEAD_DIM)
        sums = total[h : h + 1, :]
        o_ref[head, :] = (acc[head, :] / sums).astype(BF16)
        lse_ref[0, h : h + 1, :] = top[h : h + 1, :] + jnp.log2(sums)


def backward_kernel(
    me_ref, start_ref, cos_ref, sin_ref, q_ref, k_ref, v_ref, o_ref, do_ref, lse_ref,
    dq_ref, dk_ref, dv_ref, keys, values, acc, delta
):
    parts, _, chunk = k_ref.shape
    rows = q_ref.shape[1]
    me = me_ref[0]
    for part in range(parts):
        keys[part] = k_ref[part].T
        values[part] = v_ref[part].T
    start = start_ref[...]
    for h in range(RATIO):
        head = slice(h * HEAD_DIM, (h + 1) * HEAD_DIM)
        delta[h : h + 1, :] = jnp.sum(
            o_ref[head, :].astype(F32) * do_ref[head, :].astype(F32), axis=0, keepdims=True
        )

    def block(part_at, first):
        at = place_of(jnp.bitwise_xor(part_at, me), parts)
        if first:
            shown = visible(start, me * rows, part_at * chunk, chunk, rows)
        else:
            shown = (part_at * chunk + lax.broadcasted_iota(jnp.int32, (chunk, rows), 0)) >= start
        dk = dv = None
        for h in range(RATIO):
            head = slice(h * HEAD_DIM, (h + 1) * HEAD_DIM)
            query, grad = q_ref[head, :], do_ref[head, :]
            scores = dot(keys[at], query, (1,), (0,)) * score_scale_two
            scores = jnp.where(shown, scores, masked_value)
            probs = jnp.exp2(scores - lse_ref[0, h : h + 1, :])
            grad_probs = dot(values[at], grad, (1,), (0,))
            grad_scores = (probs * (grad_probs - delta[h : h + 1, :])).astype(BF16)
            dq = dot(k_ref[at], grad_scores, (1,), (0,))
            if first:
                acc[head, :] = dq
            else:
                acc[head, :] = acc[head, :] + dq
            dk_one = dot(query, grad_scores, (1,), (1,))
            dv_one = dot(grad, probs.astype(BF16), (1,), (1,))
            dk = dk_one if dk is None else dk + dk_one
            dv = dv_one if dv is None else dv + dv_one
        dk_ref[at] = (dk * score_scale).astype(BF16)
        dv_ref[at] = dv.astype(BF16)

    block(me, True)

    def later(part_at, carry):
        block(part_at, False)
        return carry

    lax.fori_loop(0, me, later, 0)

    def unseen(part_at, carry):
        at = place_of(jnp.bitwise_xor(part_at, me), parts)
        dk_ref[at] = jnp.zeros((HEAD_DIM, chunk), BF16)
        dv_ref[at] = jnp.zeros((HEAD_DIM, chunk), BF16)
        return carry

    lax.fori_loop(me + 1, parts, unseen, 0)
    cosine, sine = cos_ref[...], sin_ref[...]
    for h in range(RATIO):
        low = acc[h * HEAD_DIM : h * HEAD_DIM + HALF, :] * score_scale
        high = acc[h * HEAD_DIM + HALF : (h + 1) * HEAD_DIM, :] * score_scale
        dq_ref[h * HEAD_DIM : h * HEAD_DIM + HALF, :] = (low * cosine + high * sine).astype(BF16)
        dq_ref[h * HEAD_DIM + HALF : (h + 1) * HEAD_DIM, :] = (high * cosine - low * sine).astype(BF16)


def kernel_call(kernel, heads, ins, outs, scratch, cost):
    return pl.pallas_call(
        kernel,
        grid_spec=pltpu.PrefetchScalarGridSpec(
            num_scalar_prefetch=1, grid=(heads,), in_specs=ins,
            out_specs=[spec for spec, _ in outs], scratch_shapes=scratch,
        ),
        out_shape=[shape for _, shape in outs],
        cost_estimate=cost,
        compiler_params=pltpu.CompilerParams(vmem_limit_bytes=48 * 1024 * 1024),
    )


def attend_forward(me, start, query, keys_values, ties):
    parts, _, chunk = keys_values.shape
    rows = query.shape[1]
    group = RATIO * HEAD_DIM
    attended, totals = [], []
    for first, count in FORWARD_CALLS:
        if attended:
            me, attended[-1] = tie((me, attended[-1]), *ties[first])
        out, lse = kernel_call(
            forward_kernel,
            count,
            [
                pl.BlockSpec((1, rows), lambda g, s: (0, 0)),
                pl.BlockSpec((group, rows), lambda g, s, first=first: (g + first, 0)),
                pl.BlockSpec((parts, HEAD_DIM, chunk), lambda g, s, first=first: (0, g + first, 0)),
                pl.BlockSpec((parts, HEAD_DIM, chunk), lambda g, s, first=first: (0, KV_HEADS + g + first, 0)),
            ],
            [
                (pl.BlockSpec((group, rows), lambda g, s: (g, 0)), jax.ShapeDtypeStruct((count * group, rows), BF16)),
                (pl.BlockSpec((1, RATIO, rows), lambda g, s: (g, 0, 0)), jax.ShapeDtypeStruct((count, RATIO, rows), F32)),
            ],
            [
                pltpu.VMEM((parts, chunk, HEAD_DIM), BF16),
                pltpu.VMEM((8, rows), F32),
                pltpu.VMEM((8, rows), F32),
                pltpu.VMEM((group, rows), F32),
            ],
            SMALL,
        )(me, start, query, keys_values, keys_values)
        attended.append(out)
        totals.append(lse)
    return jnp.concatenate(attended, axis=0), jnp.concatenate(totals, axis=0)


def attend_backward(me, start, cosine, sine, query, keys_values, attended, grad_attended, totals, ties):
    parts, _, chunk = keys_values.shape
    rows = query.shape[1]
    group = RATIO * HEAD_DIM
    pieces = []
    for first, count in BACKWARD_CALLS:
        if pieces:
            me, pieces[-1] = tie((me, pieces[-1]), *ties[first])
        else:
            me = tie(me, *ties[first])
        whole = lambda g, s: (0, 0)
        by_group = lambda g, s, first=first: (g + first, 0)
        pieces.append(
            kernel_call(
                backward_kernel,
                count,
                [
                    pl.BlockSpec((1, rows), whole),
                    pl.BlockSpec((HALF, rows), whole),
                    pl.BlockSpec((HALF, rows), whole),
                    pl.BlockSpec((group, rows), by_group),
                    pl.BlockSpec((parts, HEAD_DIM, chunk), lambda g, s, first=first: (0, g + first, 0)),
                    pl.BlockSpec((parts, HEAD_DIM, chunk), lambda g, s, first=first: (0, KV_HEADS + g + first, 0)),
                    pl.BlockSpec((group, rows), by_group),
                    pl.BlockSpec((group, rows), by_group),
                    pl.BlockSpec((1, RATIO, rows), lambda g, s, first=first: (g + first, 0, 0)),
                ],
                [
                    (pl.BlockSpec((group, rows), lambda g, s: (g, 0)), jax.ShapeDtypeStruct((count * group, rows), BF16)),
                    (pl.BlockSpec((parts, HEAD_DIM, chunk), lambda g, s: (0, g, 0)), jax.ShapeDtypeStruct((parts, count * HEAD_DIM, chunk), BF16)),
                    (pl.BlockSpec((parts, HEAD_DIM, chunk), lambda g, s: (0, g, 0)), jax.ShapeDtypeStruct((parts, count * HEAD_DIM, chunk), BF16)),
                ],
                [
                    pltpu.VMEM((parts, chunk, HEAD_DIM), BF16),
                    pltpu.VMEM((parts, chunk, HEAD_DIM), BF16),
                    pltpu.VMEM((group, rows), F32),
                    pltpu.VMEM((8, rows), F32),
                ],
                SMALL,
            )(me, start, cosine, sine, query, keys_values, keys_values, attended, grad_attended, totals)
        )
    grad_query = jnp.concatenate([p[0] for p in pieces], axis=0)
    grad_keys_values = jnp.concatenate([p[1] for p in pieces] + [p[2] for p in pieces], axis=1)
    return grad_query, grad_keys_values


def feed_kernel(me_ref, x_ref, o_ref, gain_ref, dy_ref, grad_ref, *refs):
    outs, gates, ups, downs = refs[0:4], refs[4:8], refs[8:12], refs[12:16]
    (
        y_ref, h_ref, m_ref, dg_ref, du_ref, n_ref, dh_ref, dz_ref, do_ref, sums_ref,
        dx_ref, down, arrived
    ) = refs[16:]
    at = pl.program_id(0)
    me = me_ref[0]
    tile = 256
    tiles = x_ref.shape[1] // tile
    width = y_ref.shape[1]
    depth = do_ref.shape[1]

    def bring(j):
        return pltpu.make_async_copy(downs[j], down.at[j % 2], arrived.at[j % 2])

    for j in range(4):
        @pl.when(at == j)
        def _():
            if j == 0:
                bring(0).start()
            bring(j).wait()
            if j < 3:
                bring(j + 1).start()

    here = down.at[lax.rem(at, 2)]

    def rows_of(row):
        return pl.ds(pl.multiple_of(row * tile, tile), tile)

    def scale_of(hidden):
        mean = sum(jnp.sum(h * h, axis=1, keepdims=True) for h in hidden) * (1.0 / width)
        return lax.rsqrt(mean + norm_eps)

    def piece(ref):
        return ref[...].reshape(-1, ref.shape[-1])

    def before(row, carry):
        rows = rows_of(row)
        heads = [o_ref[jnp.bitwise_xor(me, k), :, rows].T for k in range(4)]
        hidden = []
        for j in range(4):
            h = x_ref[j, rows, :].astype(F32)
            for k in range(4):
                h = h + dot(heads[k], outs[k][jnp.bitwise_xor(me, j)], (1,), (1,))
            h_ref[jnp.bitwise_xor(me, j), rows, :] = h
            hidden.append(h)
        scale = scale_of(hidden)
        for j in range(4):
            n_ref[j, rows, :] = (hidden[j] * scale * gain_ref[j]).astype(BF16)
        return carry

    @pl.when(at == 0)
    def _():
        lax.fori_loop(0, tiles, before, 0)

    def some_rows(row, carry):
        rows = rows_of(row)
        gate = sum(dot(n_ref[k, rows, :], piece(gates[k]), (1,), (1,)) for k in range(4))
        up = sum(dot(n_ref[k, rows, :], piece(ups[k]), (1,), (1,)) for k in range(4))
        sigmoid = jax.nn.sigmoid(gate)
        mixed = (gate * sigmoid * up).astype(BF16)
        m_ref[0, rows, :] = mixed
        y = dot(mixed, here[...], (1,), (1,))
        grad_mixed = dot(dy_ref[rows, :], here[...], (1,), (0,))
        grad_gate = (grad_mixed * up * sigmoid * (1.0 + gate * (1.0 - sigmoid))).astype(BF16)
        grad_up = (grad_mixed * gate * sigmoid).astype(BF16)
        dg_ref[rows, :] = grad_gate
        du_ref[rows, :] = grad_up
        dx = [
            dot(grad_gate, piece(gates[k]), (1,), (0,)) + dot(grad_up, piece(ups[k]), (1,), (0,))
            for k in range(4)
        ]

        @pl.when(at == 0)
        def _():
            y_ref[rows, :] = y
            for k in range(4):
                dx_ref[k, rows, :] = dx[k]

        @pl.when(at > 0)
        def _():
            y_ref[rows, :] = y_ref[rows, :] + y
            for k in range(4):
                dx_ref[k, rows, :] = dx_ref[k, rows, :] + dx[k]

        return carry

    lax.fori_loop(0, tiles, some_rows, 0)

    def behind(row, carry):
        rows = rows_of(row)
        hidden = [h_ref[jnp.bitwise_xor(me, j), rows, :] for j in range(4)]
        scale = scale_of(hidden)
        grads = [dx_ref[j, rows, :] for j in range(4)]
        weighted = [grads[j] * gain_ref[j] for j in range(4)]
        mean = sum(
            jnp.sum(weighted[j] * hidden[j], axis=1, keepdims=True) for j in range(4)
        ) * (1.0 / width)
        cubed = scale * scale * scale * mean
        low = []
        for j in range(4):
            place = jnp.bitwise_xor(me, j)
            sums_ref[place] = sums_ref[place] + jnp.sum(grads[j] * hidden[j] * scale, axis=0, keepdims=True)
            dh = grad_ref[j, rows, :].astype(F32) + scale * weighted[j] - hidden[j] * cubed
            dh_ref[place, rows, :] = dh
            low.append(dh.astype(BF16))
            dz_ref[place, rows, :] = low[j]
        for k in range(4):
            do = sum(dot(low[j], outs[k][jnp.bitwise_xor(me, j)], (1,), (0,)) for j in range(4))
            do_ref[jnp.bitwise_xor(me, k), :, rows] = do.astype(BF16).T[:depth]
        return carry

    @pl.when(at == 3)
    def _():
        sums_ref[...] = jnp.zeros_like(sums_ref)
        lax.fori_loop(0, tiles, behind, 0)


def feed_forward(me, tokens, attended, gain, grad, grad_chunks, outs, gates, ups, downs):
    rows, width = grad.shape
    low, _, _, height, lanes = gates[0].shape
    part = downs[0].shape[1]
    ff = 4 * part
    depth = width // 4

    def held(shape):
        return pl.BlockSpec(shape, lambda j, s: (0,) * len(shape))

    def high_bits(j, s):
        chunk = jnp.bitwise_xor(s[0], j)
        return lax.div(chunk, 2), lax.rem(chunk, 2)

    def gate_place(j, s):
        highest, second = high_bits(j, s)
        return 0, second, highest, 0, 0

    def up_place(j, s):
        highest, second = high_bits(j, s)
        return second, 0, highest, 0, 0

    gate_block = pl.BlockSpec((low, 1, 1, height, lanes), gate_place)
    up_block = pl.BlockSpec((1, low, 1, height, lanes), up_place)
    wide_block = pl.BlockSpec((rows, part), lambda j, s: (0, jnp.bitwise_xor(s[0], j)))
    wide = jax.ShapeDtypeStruct((rows, ff), BF16)
    chunked = (4, rows, lanes)
    return pl.pallas_call(
        feed_kernel,
        grid_spec=pltpu.PrefetchScalarGridSpec(
            num_scalar_prefetch=1,
            grid=(4,),
            in_specs=[held(chunked), held(attended.shape), held(gain.shape), held(grad.shape), held(chunked)]
            + [held(outs[0].shape)] * 4
            + [gate_block] * 4
            + [up_block] * 4
            + [pl.BlockSpec(memory_space=pl.ANY)] * 4,
            out_specs=[
                held(grad.shape), held(chunked), pl.BlockSpec((1, rows, part), lambda j, s: (j, 0, 0)),
                wide_block, wide_block, held(chunked), held(chunked), held(chunked),
                held((4, depth, rows)), held((4, 1, lanes)),
            ],
            scratch_shapes=[
                pltpu.VMEM(chunked, F32), pltpu.VMEM((2,) + downs[0].shape, BF16), pltpu.SemaphoreType.DMA((2,))
            ],
        ),
        out_shape=[
            jax.ShapeDtypeStruct((rows, width), F32), jax.ShapeDtypeStruct(chunked, F32),
            jax.ShapeDtypeStruct((4, rows, part), BF16), wide, wide,
            jax.ShapeDtypeStruct(chunked, BF16), jax.ShapeDtypeStruct(chunked, F32),
            jax.ShapeDtypeStruct(chunked, BF16), jax.ShapeDtypeStruct((4, depth, rows), BF16),
            jax.ShapeDtypeStruct((4, 1, lanes), F32),
        ],
        cost_estimate=pl.CostEstimate(flops=12 * rows * width * ff, bytes_accessed=40_000_000, transcendentals=rows * ff),
        compiler_params=pltpu.CompilerParams(vmem_limit_bytes=58 * 1024 * 1024),
    )(me, tokens, attended, gain, grad, grad_chunks, *outs, *gates, *ups, *downs)


def rotate(values, cosine, sine):
    heads = values.reshape(-1, 2, HALF, values.shape[-1])
    low, high = heads[:, 0], heads[:, 1]
    return jnp.stack([low * cosine - high * sine, high * cosine + low * sine], axis=1).reshape(values.shape)


def rotate_back(values, cosine, sine):
    return rotate(values, cosine, -sine)


def make_layer(dp, fsdp):
    sizes = {"dp": dp, "fsdp": fsdp}
    dp_bits = [("dp", stride) for stride in strides_of(dp)]
    far, near = [("fsdp", stride) for stride in strides_of(fsdp)]
    order_one = [far] + dp_bits[::-1]
    order_two = [dp_bits[-1], far] + dp_bits[:-1][::-1]
    order_three = [dp_bits[1], far] + dp_bits[2:][::-1] + dp_bits[:1]

    def layer(
        tokens, norm_gains, query_weight, key_weight, value_weight, out_weight,
        gate_weight, up_weight, down_weight, segment_ids, out_grad
    ):
        rows = tokens.shape[0]
        cols = norm_gains.shape[1]
        depth = query_weight.shape[0]
        lanes = -(-depth // 128) * 128
        kv_cols = key_weight.shape[1]
        ff = gate_weight.shape[1] * dp
        me = lax.axis_index("fsdp").astype(jnp.int32)
        me_dp = lax.axis_index("dp").astype(jnp.int32)
        my_bits = {far: 0, near: 0}
        my_bits.update({bit: lax.rem(lax.div(me_dp, bit[1]), 2) for bit in dp_bits})


        def fill(piece):
            return jnp.pad(piece, ((0, 0), (0, -piece.shape[1] % 128)))

        def add_bits(piece, bits):
            for bit in bits:
                arrived = yield swap(piece, bit, sizes)
                piece = merge(piece, arrived, my_bits[bit] == 1)
            return piece

        def first_bits(piece):
            return add_bits(piece, dp_bits[:-1])

        last = dp_bits[-1]

        def with_last(piece, arrived):
            return merge(piece, arrived, my_bits[last] == 1)

        def spread_one(piece):
            arrived = yield swap(piece, last, sizes)
            own = with_last(piece, arrived)
            far_one, near_one = yield (swap(own, far, sizes), swap(own, near, sizes))
            both = yield swap(far_one, near, sizes)
            return [own, near_one, far_one, both]

        def spread_two(piece):
            other, side = yield (swap(piece, far, sizes), swap(piece, last, sizes))
            own = with_last(piece, side)
            other_side, near_one = yield (swap(other, last, sizes), swap(own, near, sizes))
            far_one = with_last(other, other_side)
            both = yield swap(far_one, near, sizes)
            return [own, near_one, far_one, both]

        def spread_two_late(piece):
            piece, side = yield (piece, swap(piece, last, sizes))
            own = with_last(piece, side)
            other, near_one = yield (swap(piece, far, sizes), swap(own, near, sizes))
            other_side = yield swap(other, last, sizes)
            far_one = with_last(other, other_side)
            both = yield swap(far_one, near, sizes)
            return [own, near_one, far_one, both]

        def spread_three(piece):
            own = yield from add_bits(piece, dp_bits[2:])
            other = yield swap(own, far, sizes)
            bit = dp_bits[1]
            sides = yield (swap(own, bit, sizes), swap(other, bit, sizes))
            own, far_one = [merge(p, s, my_bits[bit] == 1) for p, s in zip((own, other), sides)]
            near_one, both = yield (swap(own, near, sizes), swap(far_one, near, sizes))
            return [own, near_one, far_one, both]

        def whole_way(piece, bits, steps):
            piece = yield from add_bits(piece, bits)
            return (yield from steps(piece))

        gain_row = jnp.concatenate([norm_gains[0], norm_gains[1]])
        gain_rows = jnp.pad(gain_row[None, :], ((0, 7), (0, depth - 2 * cols)))
        kv_end = 2 * kv_cols
        own_first = fill(jnp.concatenate([query_weight.T, key_weight.T, value_weight.T, gain_rows], axis=0))
        own_second = fill(jnp.concatenate([gate_weight.T, up_weight.T], axis=0))
        own_out, own_down = fill(out_weight.T), fill(down_weight.T)

        first_chain = Chain(first_bits(own_first))
        second_chain = Chain(add_bits(own_second, dp_bits[:1]))
        while first_chain.pending is not None:
            first_chain.go_on(first_chain.pending)
            if first_chain.pending is not None:
                tie((), first_chain, second_chain)
        first = first_chain.finish()
        second = second_chain.finish()
        half = gate_weight.shape[1]
        gate_chain = Chain(whole_way(second[..., :half, :], dp_bits[1:-1], spread_two_late))
        up_chain = Chain(spread_three(second[..., half:, :]))
        own_out, own_down, first = lax.optimization_barrier((own_out, own_down, first))
        out_chain = Chain(whole_way(own_out, dp_bits[:-1], spread_one))
        down_chain = Chain(whole_way(own_down, dp_bits[:-1], spread_two))
        query_chain = Chain(spread_one(first[..., :cols, :]))
        rest_chain = Chain(spread_two(first[..., cols:, :]))
        rest = rest_chain.finish()
        rest_rows = [in_order(r, dp).reshape(dp, -1, lanes) for r in rest]
        w_key = [r[:, :kv_cols].reshape(KV_WIDTH, lanes) for r in rest_rows]
        w_value = [r[:, kv_cols:kv_end].reshape(KV_WIDTH, lanes) for r in rest_rows]
        gain_one = rest_rows[0][:, kv_end, :cols].reshape(1, D).astype(F32)
        gain_two = rest_rows[0][:, kv_end, cols : 2 * cols].reshape(1, D).astype(F32)
        w_query = [in_order(w, dp) for w in query_chain.finish()]

        ends = [jnp.sum((segment_ids < which).astype(jnp.int32)) for which in (1, 2)]
        local_ids = lax.dynamic_slice_in_dim(segment_ids, me * rows, rows)
        start = jnp.where(local_ids == 0, 0, jnp.where(local_ids == 1, ends[0], ends[1]))
        positions = me * rows + jnp.arange(rows, dtype=jnp.int32) - start
        frequency = jnp.exp(jnp.arange(HALF, dtype=F32) * (-2.0 * math.log(10000.0) / HEAD_DIM))
        angles = frequency[:, None] * positions.astype(F32)[None, :]
        cosine, sine = jnp.cos(angles), jnp.sin(angles)
        start = start[None, :]
        me_row = me[None]

        def pick(values, j):
            return lax.dynamic_index_in_dim(values, jnp.bitwise_xor(me, j), 0, keepdims=False)

        def relative_chunks(values):
            parts = values.reshape(rows, fsdp, -1).transpose(1, 0, 2)
            parts = jnp.pad(parts, ((0, 0), (0, 0), (0, -parts.shape[2] % 128)))
            return jnp.stack([pick(parts, j) for j in range(fsdp)])

        def columns_of(chunks):
            return jnp.concatenate([pick(chunks, f)[:, :depth] for f in range(fsdp)], axis=1)

        inputs = tokens.astype(F32)
        inv_one = lax.rsqrt(jnp.mean(inputs * inputs, axis=1, keepdims=True) + norm_eps)
        normed = (inputs * inv_one * gain_one).astype(BF16)
        normed_parts = relative_chunks(normed)

        def project(weight, parts):
            return sum(dot(weight[j], parts[j], (1,), (1,)) for j in range(fsdp))

        key = rotate(project(w_key, normed_parts), cosine, sine).astype(BF16)
        value = project(w_value, normed_parts).astype(BF16)
        (normed_parts, token_chunks, grad_chunks, out_grad) = tie(
            (normed_parts, relative_chunks(tokens), relative_chunks(out_grad), out_grad),
            gate_chain, up_chain, out_chain, down_chain,
        )
        query = rotate(project(w_query, normed_parts), cosine, sine).astype(BF16)
        pair = jnp.concatenate([key, value], axis=0)[None]
        far_pair = swap(pair, far, sizes)
        far_pair = tie(far_pair, gate_chain, up_chain, out_chain)
        pair = jnp.concatenate([pair, far_pair], axis=0)
        keys_values = jnp.concatenate([pair, swap(pair, near, sizes)], axis=0)
        attended, totals = attend_forward(
            me_row,
            start,
            query,
            keys_values,
            [[], [down_chain], [gate_chain, out_chain], [up_chain], [down_chain]],
        )
        attended = tie(attended, gate_chain, out_chain)
        filled = ((0, 0), (0, lanes - depth), (0, 0))
        attended_parts = jnp.pad(attended.reshape(fsdp, depth, rows), filled)
        w_out = [
            jnp.pad(in_order(w, dp).reshape(fsdp, depth, lanes), filled) for w in out_chain.finish()
        ]

        def low_bits(pieces, first):
            low = len(dp_bits) - 2
            order = list(range(pieces.ndim))
            order[first : first + low] = order[first : first + low][::-1]
            shape = list(pieces.shape)
            shape[first : first + low] = [dp // 4]
            return pieces.transpose(order).reshape(shape)

        w_gate = [low_bits(w, 0) for w in gate_chain.finish()]
        w_up = [low_bits(w, 1) for w in up_chain.finish()]
        w_down = [in_order(w, dp) for w in down_chain.finish()]

        attended_own = jnp.stack([pick(attended_parts, j) for j in range(fsdp)])
        gain_own = relative_chunks(jnp.broadcast_to(gain_two, (rows, D)))[:, :1]
        fed, hidden, mixed, grad_gate, grad_up, two_own, grad_hidden, branch_grad, grad_attended, gain_sums = (
            feed_forward(
                me_row, token_chunks, attended_parts, gain_own, out_grad,
                grad_chunks, w_out, w_gate, w_up, w_down
            )
        )
        grad_attended = grad_attended.reshape(D, rows)


        def halves_of(right_own):
            return [jnp.concatenate([right_own[w], right_own[w + 2]], axis=1) for w in (1, 0)]

        def start_sum(sent, kept, order):
            return Chain(summed(sent, kept, dp_bits + [far], near, order, sizes, my_bits))

        def product_sum(left, right_own, order, contract=(0,)):
            sent, kept = [dot(left, r, contract, (0,)).astype(BF16) for r in halves_of(right_own)]
            return start_sum(sent, kept, order)

        sum_down = product_sum(out_grad, mixed, order_one)
        sum_gate = product_sum(grad_gate, two_own, order_two)
        sum_up = product_sum(grad_up, two_own, order_three)
        def out_product(right):
            whole = lax.dot_general(
                branch_grad, right, (((1,), (0,)), ((), ())), preferred_element_type=F32
            )
            return whole[:, :depth].astype(BF16).reshape(D, right.shape[1])

        sum_out = start_sum(
            *[out_product(r) for r in halves_of(attended_own.transpose(0, 2, 1))], order_two
        )

        early = [sum_down, sum_gate, sum_up, sum_out]
        grad_query, grad_keys_values = attend_backward(
            me_row, start, cosine, sine, query, keys_values, attended, grad_attended, totals,
            [early, [], early, [], [sum_down, sum_gate]],
        )
        sum_query = product_sum(grad_query, normed_parts, order_two, (1,))

        near_kv = swap(grad_keys_values[2:], near, sizes)
        near_kv, hidden, fed, grad_hidden, gain_sums = tie(
            (near_kv, hidden, fed, grad_hidden, gain_sums), sum_query, sum_up
        )
        far_kv = swap(
            (grad_keys_values[1].astype(F32) + near_kv[1].astype(F32)).astype(BF16), far, sizes
        )
        far_kv = tie(far_kv, sum_query, sum_gate, sum_out, sum_down, sum_up)

        def plain(chunks):
            return jnp.concatenate([chunks[f][:, :depth] for f in range(fsdp)], axis=1)

        output = plain(hidden) + fed
        grad_hidden = plain(grad_hidden)
        grad_gain_two = plain(gain_sums).reshape(D)
        key_value_sum = (
            grad_keys_values[0].astype(F32) + near_kv[0].astype(F32) + far_kv.astype(F32)
        )
        grad_key = rotate_back(key_value_sum[:KV_WIDTH], cosine, sine).astype(BF16)
        grad_value = key_value_sum[KV_WIDTH:].astype(BF16)
        grad_normed = columns_of(
            jnp.stack(
                [
                    dot(grad_query, w_query[j], (0,), (0,))
                    + dot(grad_key, w_key[j], (0,), (0,))
                    + dot(grad_value, w_value[j], (0,), (0,))
                    for j in range(fsdp)
                ]
            )
        )
        weighted_one = grad_normed * gain_one
        grad_gain_one = jnp.sum(grad_normed * inputs * inv_one, axis=0)
        input_grad = (
            grad_hidden
            + inv_one * weighted_one
            - inputs * (inv_one * inv_one * inv_one) * jnp.mean(weighted_one * inputs, axis=1, keepdims=True)
        )
        both = jnp.concatenate(
            [grad_key.reshape(dp, kv_cols, rows), grad_value.reshape(dp, kv_cols, rows)], axis=1
        ).reshape(dp * kv_end, rows)
        gains_piece = jnp.concatenate(
            [grad_gain_one.reshape(dp, 1, cols), grad_gain_two.reshape(dp, 1, cols)], axis=2
        )
        gains_piece = fill(
            jnp.pad(gains_piece, ((0, 0), (0, 7), (0, 0))).reshape(dp * 8, 2 * cols)
        ).astype(BF16)
        gains_piece = jnp.pad(gains_piece, ((0, 0), (0, lanes - gains_piece.shape[1]))).reshape(dp, 8, lanes)
        gains_piece = jnp.concatenate([gains_piece, gains_piece], axis=2)
        sent, kept = [
            jnp.concatenate([dot(both, r, (1,), (0,)).astype(BF16).reshape(dp, kv_end, 2 * lanes), gains_piece], axis=1)
            for r in halves_of(normed_parts)
        ]
        last_chain = start_sum(sent, kept, order_one)
        tie((), last_chain, sum_query)
        tie((), last_chain, sum_query, sum_gate, sum_out, sum_down, sum_up)
        while last_chain.pending is not None:
            tie((), last_chain, sum_query)
        last_sum = last_chain.result
        out_down, out_gate, out_up, out_out, out_query = [
            chain.finish() for chain in (sum_down, sum_gate, sum_up, sum_out, sum_query)
        ]
        return (
            output.astype(BF16),
            input_grad,
            last_sum[kv_end, : 2 * cols].reshape(2, cols),
            out_query[:, :depth].T,
            last_sum[:kv_cols, :depth].T,
            last_sum[kv_cols:kv_end, :depth].T,
            out_out[:, :depth].T,
            out_gate[:, :depth].T,
            out_up[:, :depth].T,
            out_down.T,
        )

    return layer


def solution(mesh):
    weight = P("fsdp", "dp")
    token = P(("dp", "fsdp"), None)
    gains = P(None, "dp")
    return jax.shard_map(
        make_layer(mesh.shape["dp"], mesh.shape["fsdp"]),
        mesh=mesh,
        in_specs=(token, gains) + (weight,) * 7 + (P("dp"), token),
        out_specs=(token, token, gains) + (weight,) * 7,
        check_vma=False,
    )
```
